32 devices in a mesh: dp: 8 (over z, core), fsdp: 4 (over y, x).
Axes of the slice: x: 2, y: 2, z: 4, core: 2. Of those that a mesh axis runs over, the one named last changes fastest.
Arguments:
- node: float32 [128, 32, 256], P(('dp', 'fsdp')), may hold values from -6 to 6
- edge: float32 [128, 32, 32, 128], P(('dp', 'fsdp')), may hold values from -6 to 6
- rotvec: float32 [128, 3, 32], P(('dp', 'fsdp')), may hold values from -6 to 6
- trans: float32 [128, 3, 32], P(('dp', 'fsdp')), may hold values from -6 to 6
- chain: int32 [128, 32], P(('dp', 'fsdp')), may hold values from 0 to 3, never falling along the last dimension, each value on 1 to 16 neighbouring positions
- timestep: int32 [128], P(('dp', 'fsdp')), may hold values from 1 to 999
- ipa_params: float32 [2705408], P(('dp', 'fsdp')), may hold values from -4 to 4
- rest_params: float32 [1912832], P(('dp', 'fsdp')), may hold values from -4 to 4
- node_cot: float32 [128, 32, 256], P(('dp', 'fsdp')), may hold values from -6 to 6
- edge_cot: float32 [128, 32, 32, 128], P(('dp', 'fsdp')), may hold values from -6 to 6
- rot_cot: float32 [128, 9, 32], P(('dp', 'fsdp')), may hold values from -6 to 6
- trans_cot: float32 [128, 3, 32], P(('dp', 'fsdp')), may hold values from -6 to 6
Outputs:
- node_out: float32 [128, 32, 256], P(('dp', 'fsdp'))
- edge_out: float32 [128, 32, 32, 128], P(('dp', 'fsdp'))
- rot_out: float32 [128, 9, 32], P(('dp', 'fsdp'))
- trans_out: float32 [128, 3, 32], P(('dp', 'fsdp'))
- node_grad: float32 [128, 32, 256], P(('dp', 'fsdp'))
- edge_grad: float32 [128, 32, 32, 128], P(('dp', 'fsdp'))
- rotvec_grad: float32 [128, 3, 32], P(('dp', 'fsdp'))
- trans_grad: float32 [128, 3, 32], P(('dp', 'fsdp'))
- ipa_grad: float32 [2705408], P(('dp', 'fsdp'))
- rest_grad: float32 [1912832], P(('dp', 'fsdp'))
The draws below stay inside these ranges and needn't reach their ends.
Inputs may be any that keep to these rules, and one draw needn't show every extreme that they name: Each crop's chain index never falls, every chain of 0 to 3 occurs, each with 1 to 16 residues.
All inputs are finite; a program needn't handle non-finite values.
Results may differ from the reference program's by a relative error of at most 0.0003.
Values sent between devices are 32-bit elements; how exact they have to be, the bound alone decides.
A program may use at most 256 MiB of HBM per device.

```python
import math
import jax
import jax.numpy as jnp
import numpy as np
from jax import lax

D = 256
E = 128
HEADS = 8
HEAD_DIM = 256
QPTS = 8
VPTS = 12
SKIP = 64
TF_HEADS = 4
LEN = 32
CHAINS = 4
CROPS = 128
P_IPA = 2705408
P_REST = 1912832


def with_ends(array, stream_key, least, high):
    place = [jax.random.randint(jax.random.fold_in(stream_key, axis), (), 0, length) for axis, length in enumerate(array.shape)]
    main_axis = array.shape.index(max(array.shape))
    beside = place[:main_axis] + [(place[main_axis] + 1) % array.shape[main_axis]] + place[main_axis + 1:]
    return array.at[tuple(place)].set(least).at[tuple(beside)].set(high)


def shard_levels(stream_key, shape, cuts, low, largest):
    level = 1.0
    for position, parts in cuts:
        draws = jax.random.uniform(jax.random.fold_in(jax.random.fold_in(stream_key, 6), position), (parts,), jnp.float32, low / len(cuts), largest / len(cuts))
        level = level * jnp.repeat(jnp.exp(draws), shape[position] // parts).reshape((-1,) + (1,) * (len(shape) - 1 - position))
    return level


def split_up(number_of, total, bound, slope):
    weights = [(1 << 20) // math.isqrt(rank ** slope) + 1 for rank in range(2, number_of + 1)]
    rest, holding = total - bound - (number_of - 1), [1] * (number_of - 1)
    while rest > 0:
        candidates = [i for i in range(number_of - 1) if holding[i] < bound]
        whole, budget = sum([weights[i] for i in candidates]), rest
        for i in candidates:
            more = min(bound - holding[i], max(1, budget * weights[i] // whole), rest)
            holding[i] = holding[i] + more
            rest = rest - more
    return np.array([bound] + holding)


def uneven_parts(own_key, number_of, total, reach, lean):
    if number_of == 2:
        one = jax.random.randint(own_key, (), max(1, total - reach), min(reach, total - 1) + 1)
        return jnp.stack([one, total - one])
    sizes = jnp.asarray(split_up(number_of, total, reach, lean), jnp.int32)
    twos = (number_of - 1) // 2
    donor, taker = sizes[1:1 + 2 * twos:2], sizes[2:2 + 2 * twos:2]
    room = jnp.minimum(donor - 1, reach - taker)
    passed = jax.random.randint(jax.random.fold_in(own_key, 1), (twos,), 0, 1 << 20) % (room + 1)
    sizes = sizes.at[1:1 + 2 * twos:2].set(donor - passed).at[2:2 + 2 * twos:2].set(taker + passed)
    return sizes[jax.random.permutation(jax.random.fold_in(own_key, 2), number_of)]


def centred(stream_key, dims, scale, bound, cuts=(), held_as=jnp.bfloat16):
    values = scale * jax.random.normal(stream_key, dims, jnp.float32)
    if cuts:
        values = values * shard_levels(stream_key, dims, cuts, -0.22, 0.18)
    return jnp.clip(values, -bound, bound).astype(held_as)


def setup_inputs(seed: int = 0) -> dict:
    arg_keys = jax.random.split(jax.random.key(seed), 13)
    return {
        "node": centred(arg_keys[0], (CROPS, LEN, D), 1.0, 6.0, ((0, 32),), jnp.float32),
        "edge": centred(arg_keys[1], (CROPS, LEN, LEN, E), 1.0, 6.0, ((0, 32),), jnp.float32),
        "rotvec": centred(arg_keys[2], (CROPS, 3, LEN), 1.0, 6.0, ((0, 32),), jnp.float32),
        "trans": centred(arg_keys[3], (CROPS, 3, LEN), 1.0, 6.0, ((0, 32),), jnp.float32),
        "chain": jax.vmap(lambda own: jnp.searchsorted(jnp.cumsum(uneven_parts(own, CHAINS, LEN, LEN // 2, 1)), jnp.arange(LEN), side="right"))(jax.random.split(arg_keys[4], CROPS)).reshape((CROPS, LEN)).astype(jnp.int32),
        "timestep": with_ends(jax.random.randint(arg_keys[5], (CROPS,), 1, 1000), jax.random.fold_in(arg_keys[5], 1), 1, 999).astype(jnp.int32),
        "ipa_params": centred(arg_keys[6], (P_IPA,), 1.0, 4.0, ((0, 32),), jnp.float32),
        "rest_params": centred(arg_keys[7], (P_REST,), 1.0, 4.0, ((0, 32),), jnp.float32),
        "node_cot": centred(arg_keys[8], (CROPS, LEN, D), 1.0, 6.0, ((0, 32),), jnp.float32),
        "edge_cot": centred(arg_keys[9], (CROPS, LEN, LEN, E), 1.0, 6.0, ((0, 32),), jnp.float32),
        "rot_cot": centred(arg_keys[10], (CROPS, 9, LEN), 1.0, 6.0, ((0, 32),), jnp.float32),
        "trans_cot": centred(arg_keys[11], (CROPS, 3, LEN), 1.0, 6.0, ((0, 32),), jnp.float32),
    }


highest = lax.Precision.HIGHEST

def matmul(left, right):
    return jnp.dot(left, right, precision=highest)

def ipa_table():
    point_q = HEADS * QPTS * 3
    point_v = HEADS * VPTS * 3
    joined_width = HEADS * HEAD_DIM + point_v + HEADS * VPTS + HEADS * E
    scalar_width = HEADS * HEAD_DIM
    return (('time_w', (D, D), 'weight'), ('ipa_gain', (D,), 'gain'), ('ipa_shift', (D,), 'bias'), ('query_w', (D, scalar_width), 'weight'), ('query_b', (scalar_width,), 'bias'), ('key_w', (D, scalar_width), 'weight'), ('key_b', (scalar_width,), 'bias'), ('value_w', (D, scalar_width), 'weight'), ('value_b', (scalar_width,), 'bias'), ('qpoint_w', (D, point_q), 'weight'), ('qpoint_b', (point_q,), 'bias'), ('kpoint_w', (D, point_q), 'weight'), ('kpoint_b', (point_q,), 'bias'), ('vpoint_w', (D, point_v), 'weight'), ('vpoint_b', (point_v,), 'bias'), ('pair_w', (E, HEADS), 'weight'), ('pair_b', (HEADS,), 'bias'), ('head_w', (HEADS,), 'plain'), ('out_w', (joined_width, D), 'output'), ('out_b', (D,), 'bias'))

def rest_table():
    width = D + SKIP
    entries = (('skip_w', (D, SKIP), 'weight'), ('skip_b', (SKIP,), 'bias'))
    for layer_tag in ('0', '1'):
        entries = entries + (('attn_in_w' + layer_tag, (width, 3 * width), 'weight'), ('attn_in_b' + layer_tag, (3 * width,), 'bias'), ('attn_out_w' + layer_tag, (width, width), 'output'), ('attn_out_b' + layer_tag, (width,), 'bias'), ('first_gain' + layer_tag, (width,), 'gain'), ('first_shift' + layer_tag, (width,), 'bias'), ('ff_one_w' + layer_tag, (width, width), 'weight'), ('ff_one_b' + layer_tag, (width,), 'bias'), ('ff_two_w' + layer_tag, (width, width), 'weight'), ('ff_two_b' + layer_tag, (width,), 'bias'), ('second_gain' + layer_tag, (width,), 'gain'), ('second_shift' + layer_tag, (width,), 'bias'))
    entries = entries + (('post_w', (width, D), 'weight'), ('post_b', (D,), 'bias'), ('trans_one_w', (D, D), 'weight'), ('trans_one_b', (D,), 'bias'), ('trans_two_w', (D, D), 'weight'), ('trans_two_b', (D,), 'bias'), ('trans_three_w', (D, D), 'weight'), ('trans_three_b', (D,), 'bias'), ('trans_gain', (D,), 'gain'), ('trans_shift', (D,), 'bias'), ('backbone_w', (D, 6), 'weight'), ('backbone_b', (6,), 'bias'), ('edge_node_w', (D, E), 'weight'), ('edge_node_b', (E,), 'bias'), ('edge_one_w', (3 * E, 3 * E), 'weight'), ('edge_one_b', (3 * E,), 'bias'), ('edge_two_w', (3 * E, 3 * E), 'weight'), ('edge_two_b', (3 * E,), 'bias'), ('edge_final_w', (3 * E, E), 'weight'), ('edge_final_b', (E,), 'bias'), ('edge_gain', (E,), 'gain'), ('edge_shift', (E,), 'bias'))
    return entries

def unpack(flat_params, param_table):
    params = {}
    offset = 0
    for entry_name, entry_shape, entry_kind in param_table:
        entry_count = math.prod(entry_shape)
        segment_part = flat_params[offset:offset + entry_count].reshape(entry_shape)
        offset = offset + entry_count
        if entry_kind == 'weight':
            segment_part = segment_part * entry_shape[0] ** (-0.5)
        elif entry_kind == 'output':
            segment_part = segment_part * (2.0 * entry_shape[0] ** (-0.5))
        elif entry_kind == 'bias':
            segment_part = segment_part * 0.1
        elif entry_kind == 'gain':
            segment_part = 1.0 + 0.1 * segment_part
        params[entry_name] = segment_part
    return params

def layer_norm(values, gain, shift):
    centered = values - lax.optimization_barrier(jnp.mean(values, -1, keepdims=True))
    spread = lax.optimization_barrier(jnp.mean(centered * centered, -1, keepdims=True))
    return centered * lax.rsqrt(spread + 1e-05) * gain + shift

def rotation(vector):
    norm_scale = lax.rsqrt(1.0 + lax.optimization_barrier(jnp.sum(vector * vector, 0)))
    comp_a = norm_scale
    comp_b = vector[0] * norm_scale
    comp_c = vector[1] * norm_scale
    comp_d = vector[2] * norm_scale
    entries = [comp_a * comp_a + comp_b * comp_b - comp_c * comp_c - comp_d * comp_d, 2.0 * (comp_b * comp_c - comp_a * comp_d), 2.0 * (comp_b * comp_d + comp_a * comp_c), 2.0 * (comp_b * comp_c + comp_a * comp_d), comp_a * comp_a - comp_b * comp_b + comp_c * comp_c - comp_d * comp_d, 2.0 * (comp_c * comp_d - comp_a * comp_b), 2.0 * (comp_b * comp_d - comp_a * comp_c), 2.0 * (comp_c * comp_d + comp_a * comp_b), comp_a * comp_a - comp_b * comp_b - comp_c * comp_c + comp_d * comp_d]
    return jnp.stack(entries).reshape(3, 3, -1)

def points_of(node_in, weight, bias, point_count):
    flat_points = matmul(node_in, weight) + bias
    return flat_points.reshape(node_in.shape[0], 3, HEADS, point_count).transpose(1, 0, 2, 3)

def to_global(frame_rot, frame_shift, local_points):
    moved = jnp.einsum('cdl,dlhp->clhp', frame_rot, local_points, precision=highest)
    return moved + frame_shift[:, :, None, None]

def point_attention(params, node_in, edge_in, frame_rot, frame_shift, same_chain):
    length = node_in.shape[0]
    query_rows = (matmul(node_in, params['query_w']) + params['query_b']).reshape(length, HEADS, HEAD_DIM)
    key_rows = (matmul(node_in, params['key_w']) + params['key_b']).reshape(length, HEADS, HEAD_DIM)
    value_rows = (matmul(node_in, params['value_w']) + params['value_b']).reshape(length, HEADS, HEAD_DIM)
    query_pts = to_global(frame_rot, frame_shift, points_of(node_in, params['qpoint_w'], params['qpoint_b'], QPTS))
    key_pts = to_global(frame_rot, frame_shift, points_of(node_in, params['kpoint_w'], params['kpoint_b'], QPTS))
    value_pts = to_global(frame_rot, frame_shift, points_of(node_in, params['vpoint_w'], params['vpoint_b'], VPTS))
    pair_bias = jnp.einsum('ijf,fh->hij', edge_in, params['pair_w'], precision=highest) + params['pair_b'][:, None, None]
    scalar_term = jnp.einsum('ihc,jhc->hij', query_rows, key_rows, precision=highest) * HEAD_DIM ** (-0.5)
    query_sq = lax.optimization_barrier(jnp.sum(query_pts * query_pts, (0, 3))).T
    key_sq = lax.optimization_barrier(jnp.sum(key_pts * key_pts, (0, 3))).T
    cross_term = jnp.einsum('cihp,cjhp->hij', query_pts, key_pts, precision=highest)
    distance = query_sq[:, :, None] + key_sq[:, None, :] - 2.0 * cross_term
    point_weight = jax.nn.softplus(params['head_w']) * (math.sqrt(2.0 / (9.0 * QPTS)) / 2.0)
    logits = math.sqrt(1.0 / 3.0) * (scalar_term + pair_bias - point_weight[:, None, None] * distance)
    logits = jnp.where(same_chain[None], logits, -1000000000.0)
    attend = jax.nn.softmax(logits, axis=-1)
    scalar_out = jnp.einsum('hij,jhc->ihc', attend, value_rows, precision=highest).reshape(length, -1)
    point_out = jnp.einsum('hij,cjhp->cihp', attend, value_pts, precision=highest)
    local_out = jnp.einsum('dcl,dlhp->clhp', frame_rot, point_out - frame_shift[:, :, None, None], precision=highest)
    point_norm = jnp.sqrt(lax.optimization_barrier(jnp.sum(local_out * local_out, 0)) + 1.0)
    pair_out = jnp.einsum('hij,ijf->ihf', attend, edge_in, precision=highest).reshape(length, -1)
    joined = jnp.concatenate([scalar_out, local_out.transpose(1, 0, 2, 3).reshape(length, -1), point_norm.reshape(length, -1), pair_out], -1)
    return matmul(joined, params['out_w']) + params['out_b']

def encoder_block(params, layer_tag, hidden_in, same_chain):
    length = hidden_in.shape[0]
    width = hidden_in.shape[1]
    head_size = width // TF_HEADS
    packed = matmul(hidden_in, params['attn_in_w' + layer_tag]) + params['attn_in_b' + layer_tag]
    query_rows = packed[:, :width].reshape(length, TF_HEADS, head_size)
    key_rows = packed[:, width:2 * width].reshape(length, TF_HEADS, head_size)
    value_rows = packed[:, 2 * width:].reshape(length, TF_HEADS, head_size)
    scores = jnp.einsum('ihc,jhc->hij', query_rows, key_rows, precision=highest) * head_size ** (-0.5)
    scores = jnp.where(same_chain[None], scores, -1000000000.0)
    weights = jax.nn.softmax(scores, axis=-1)
    mixed_heads = jnp.einsum('hij,jhc->ihc', weights, value_rows, precision=highest).reshape(length, width)
    attended = matmul(mixed_heads, params['attn_out_w' + layer_tag]) + params['attn_out_b' + layer_tag]
    normed = layer_norm(hidden_in + attended, params['first_gain' + layer_tag], params['first_shift' + layer_tag])
    inner_act = jax.nn.gelu(matmul(normed, params['ff_one_w' + layer_tag]) + params['ff_one_b' + layer_tag])
    feed = matmul(inner_act, params['ff_two_w' + layer_tag]) + params['ff_two_b' + layer_tag]
    return layer_norm(normed + feed, params['second_gain' + layer_tag], params['second_shift' + layer_tag])

def edge_update(params, node_in, edge_in):
    length = node_in.shape[0]
    projected = matmul(node_in, params['edge_node_w']) + params['edge_node_b']
    joined = jnp.concatenate([edge_in, jnp.broadcast_to(projected[:, None, :], (length, length, E)), jnp.broadcast_to(projected[None, :, :], (length, length, E))], -1)
    joined = joined.reshape(length * length, 3 * E)
    first_layer = jax.nn.gelu(matmul(joined, params['edge_one_w']) + params['edge_one_b'])
    second_layer = jax.nn.gelu(matmul(first_layer, params['edge_two_w']) + params['edge_two_b'])
    result = matmul(second_layer + joined, params['edge_final_w']) + params['edge_final_b']
    return layer_norm(result, params['edge_gain'], params['edge_shift']).reshape(length, length, E)

def whole_layer(ipa_flat, rest_flat, node_in, edge_in, quat_vec, shift_in, chain_ids, step_value):
    ipa_prm = unpack(ipa_flat, ipa_table())
    rest_prm = unpack(rest_flat, rest_table())
    same_chain = chain_ids[:, None] == chain_ids[None, :]
    half_width = D // 2
    frequency = jnp.exp(-math.log(10000.0) * jnp.arange(half_width, dtype=jnp.float32) / half_width)
    angles = step_value.astype(jnp.float32) * frequency
    embedded = jnp.concatenate([jnp.sin(angles), jnp.cos(angles)])
    node_time = node_in + matmul(embedded[None, :], ipa_prm['time_w'])
    frame_rot = rotation(quat_vec)
    attended = point_attention(ipa_prm, node_time, edge_in, frame_rot, shift_in, same_chain)
    node_ipa = layer_norm(node_time + attended, ipa_prm['ipa_gain'], ipa_prm['ipa_shift'])
    skipped = matmul(node_in, rest_prm['skip_w']) + rest_prm['skip_b']
    encoded = jnp.concatenate([node_ipa, skipped], -1)
    for layer_tag in ('0', '1'):
        encoded = encoder_block(rest_prm, layer_tag, encoded, same_chain)
    node_mid = node_ipa + matmul(encoded, rest_prm['post_w']) + rest_prm['post_b']
    inner_act = jax.nn.gelu(matmul(node_mid, rest_prm['trans_one_w']) + rest_prm['trans_one_b'])
    inner_act = jax.nn.gelu(matmul(inner_act, rest_prm['trans_two_w']) + rest_prm['trans_two_b'])
    feed = matmul(inner_act, rest_prm['trans_three_w']) + rest_prm['trans_three_b']
    node_out = layer_norm(node_mid + feed, rest_prm['trans_gain'], rest_prm['trans_shift'])
    update = matmul(node_out, rest_prm['backbone_w']) + rest_prm['backbone_b']
    update_rot = rotation(update[:, :3].T)
    new_rot = jnp.einsum('cdl,del->cel', frame_rot, update_rot, precision=highest)
    new_shift = jnp.einsum('cdl,dl->cl', frame_rot, update[:, 3:].T, precision=highest) + shift_in
    edge_out = edge_update(rest_prm, node_out, edge_in)
    return (node_out, edge_out, new_rot.reshape(9, -1), new_shift)

def reference(node, edge, rotvec, trans, chain, timestep, ipa_params, rest_params, node_cot, edge_cot, rot_cot, trans_cot):

    def one_crop(totals, crop_data):
        node_in, edge_in, quat_vec, shift_in, chain_ids, step_value, cot_node, cot_edge, cot_rot, cot_shift = crop_data

        def forward(ipa_flat, rest_flat, node_x, edge_x, quat_x, shift_x):
            return whole_layer(ipa_flat, rest_flat, node_x, edge_x, quat_x, shift_x, chain_ids, step_value)
        results, pullback = jax.vjp(forward, ipa_params, rest_params, node_in, edge_in, quat_vec, shift_in)
        gradients = pullback((cot_node, cot_edge, cot_rot, cot_shift))
        new_totals = (totals[0] + gradients[0], totals[1] + gradients[1])
        return (new_totals, (results[0], results[1], results[2], results[3], gradients[2], gradients[3], gradients[4], gradients[5]))
    initial = (jnp.zeros_like(ipa_params), jnp.zeros_like(rest_params))
    totals, stacked = lax.scan(one_crop, initial, (node, edge, rotvec, trans, chain, timestep, node_cot, edge_cot, rot_cot, trans_cot))
    return (stacked[0], stacked[1], stacked[2], stacked[3], stacked[4], stacked[5], stacked[6], stacked[7], totals[0], totals[1])
```

```python
import math
from types import SimpleNamespace
from typing import Any, NamedTuple

import jax
import jax.numpy as jnp
from jax import lax
from jax.experimental import pallas as pl
from jax.experimental.pallas import tpu as pltpu
from jax.sharding import PartitionSpec as P

D = 256
E = 128
HEADS = 8
HEAD_DIM = 256
QPTS = 8
VPTS = 12
SKIP = 64
TF_HEADS = 4
WIDTH = D + SKIP

WEIGHT, OUTPUT, BIAS, GAIN, PLAIN = range(5)
AXES = ("dp", "fsdp")


def ipa_table():
    point_q = HEADS * QPTS * 3
    point_v = HEADS * VPTS * 3
    scalar = HEADS * HEAD_DIM
    joined = scalar + point_v + HEADS * VPTS + HEADS * E
    return dict(
        time_w=((D, D), WEIGHT),
        ipa_gain=((D,), GAIN),
        ipa_shift=((D,), BIAS),
        query_w=((D, scalar), WEIGHT),
        query_b=((scalar,), BIAS),
        key_w=((D, scalar), WEIGHT),
        key_b=((scalar,), BIAS),
        value_w=((D, scalar), WEIGHT),
        value_b=((scalar,), BIAS),
        qpoint_w=((D, point_q), WEIGHT),
        qpoint_b=((point_q,), BIAS),
        kpoint_w=((D, point_q), WEIGHT),
        kpoint_b=((point_q,), BIAS),
        vpoint_w=((D, point_v), WEIGHT),
        vpoint_b=((point_v,), BIAS),
        pair_w=((E, HEADS), WEIGHT),
        pair_b=((HEADS,), BIAS),
        head_w=((HEADS,), PLAIN),
        out_w=((joined, D), OUTPUT),
        out_b=((D,), BIAS),
    )


def rest_table():
    square, vector = ((WIDTH, WIDTH), WEIGHT), ((WIDTH,), BIAS)
    packed, packed_bias = ((WIDTH, 3 * WIDTH), WEIGHT), ((3 * WIDTH,), BIAS)
    mixing, gains = ((WIDTH, WIDTH), OUTPUT), ((WIDTH,), GAIN)
    return dict(
        skip_w=((D, SKIP), WEIGHT),
        skip_b=((SKIP,), BIAS),
        attn_in_w0=packed,
        attn_in_b0=packed_bias,
        attn_out_w0=mixing,
        attn_out_b0=vector,
        first_gain0=gains,
        first_shift0=vector,
        ff_one_w0=square,
        ff_one_b0=vector,
        ff_two_w0=square,
        ff_two_b0=vector,
        second_gain0=gains,
        second_shift0=vector,
        attn_in_w1=packed,
        attn_in_b1=packed_bias,
        attn_out_w1=mixing,
        attn_out_b1=vector,
        first_gain1=gains,
        first_shift1=vector,
        ff_one_w1=square,
        ff_one_b1=vector,
        ff_two_w1=square,
        ff_two_b1=vector,
        second_gain1=gains,
        second_shift1=vector,
        post_w=((WIDTH, D), WEIGHT),
        post_b=((D,), BIAS),
        trans_one_w=((D, D), WEIGHT),
        trans_one_b=((D,), BIAS),
        trans_two_w=((D, D), WEIGHT),
        trans_two_b=((D,), BIAS),
        trans_three_w=((D, D), WEIGHT),
        trans_three_b=((D,), BIAS),
        trans_gain=((D,), GAIN),
        trans_shift=((D,), BIAS),
        backbone_w=((D, 6), WEIGHT),
        backbone_b=((6,), BIAS),
        edge_node_w=((D, E), WEIGHT),
        edge_node_b=((E,), BIAS),
        edge_one_w=((3 * E, 3 * E), WEIGHT),
        edge_one_b=((3 * E,), BIAS),
        edge_two_w=((3 * E, 3 * E), WEIGHT),
        edge_two_b=((3 * E,), BIAS),
        edge_final_w=((3 * E, E), WEIGHT),
        edge_final_b=((E,), BIAS),
        edge_gain=((E,), GAIN),
        edge_shift=((E,), BIAS),
    )


EDGE_NAMES = tuple(list(rest_table())[-8:])


LANES = 128
MESH = pl.DeviceIdType.MESH
VMEM_LIMIT = 62 * 1024 * 1024


def up_to(count, step):
    return -(-count // step) * step


def layout(table):
    entries = []
    offset = 0
    for name, (shape, kind) in table.items():
        rows, width = shape if len(shape) == 2 else (1, shape[0])
        scale = {WEIGHT: shape[0] ** (-0.5), OUTPUT: 2.0 * shape[0] ** (-0.5), PLAIN: 1.0}.get(kind, 0.1)
        entries.append((name, offset, rows, width, scale, 1.0 if kind == GAIN else 0.0))
        offset = offset + rows * width
    return entries


def pieces(offset, rows, width):
    period = LANES // math.gcd(width, LANES)
    if rows % period:
        period = rows
    count = rows // period
    stride = period * width // LANES
    for column in range(0, width, LANES):
        used = min(LANES, width - column)
        starts = [offset + first * width + column for first in range(period)]
        places = [(first, start // LANES, start % LANES) for first, start in enumerate(starts)]
        yield column, used, period, count, stride, places


def row_slice(start, count, stride):
    return pl.ds(start, count, stride=stride) if count > 1 and stride > 1 else pl.ds(start, count)


def unpack_into(flat, entries, outs, stage):
    for name, offset, rows, width, scale, shift in entries:
        out = outs[name]
        for column, used, period, count, stride, places in pieces(offset, rows, width):
            for first, row, lane in places:
                tile = flat[row_slice(row, count, stride), :]
                at = lax.broadcasted_iota(jnp.int32, tile.shape, 1)
                if lane:
                    tile = pltpu.roll(tile, LANES - lane, 1)
                    if lane + used > LANES:
                        after = pltpu.roll(flat[row_slice(row + 1, count, stride), :], LANES - lane, 1)
                        tile = jnp.where(at < LANES - lane, tile, after)
                tile = tile * scale + shift if shift else tile * scale
                if used < LANES:
                    tile = jnp.where(at < used, tile, 0.0)
                if period == 1:
                    out[:, column : column + LANES] = tile
                else:
                    stage[row_slice(first, count, period), :] = tile
            if period > 1:
                out[:, column : column + LANES] = stage[0:rows, :]


def pack_into(flat, entries, grads, stage):
    for name, offset, rows, width, scale, _ in entries:
        held = grads[name]
        for column, used, period, count, stride, places in pieces(offset, rows, width):
            if period > 1:
                stage[0:rows, :] = held[:, column : column + LANES]
            for first, row, lane in places:
                if period == 1:
                    tile = held[:, column : column + LANES] * scale
                else:
                    tile = stage[row_slice(first, count, period), :] * scale
                at = lax.broadcasted_iota(jnp.int32, tile.shape, 1)
                if lane:
                    tile = pltpu.roll(tile, lane, 1)
                here = row_slice(row, count, stride)
                if lane == 0 and used == LANES:
                    flat[here, :] = tile
                    continue
                flat[here, :] = jnp.where((at >= lane) & (at < lane + used), tile, flat[here, :])
                if lane + used > LANES:
                    after = row_slice(row + 1, count, stride)
                    flat[after, :] = jnp.where(at < lane + used - LANES, tile, flat[after, :])


def ring_place(turn):
    return turn + (turn // 2) * (5 - 2 * turn)


PAIR_ROWS = 1321
EVEN_ROWS, ODD_ROWS = 661, 660


PARTS = (0, 1, 2)
REST = 2
CUT = 336


def by_line(part, up):
    return up != 0 if part == REST else abs(up) == 1


def hops():
    order = [
        (abs(up) + abs(side) + 3 * (part // REST), part, abs(up), up, side)
        for part in PARTS
        for up in range(-3, 4)
        for side in (0, 1, -1, 2)
    ]
    return [(part, up, side) for _, part, _, up, side in sorted(order)]


class Gather:
    def __init__(self, ipa_flat, rest_flat, send_sem, recv_sem, pair_send, pair_recv):
        self.flats = (ipa_flat, rest_flat)
        self.sems = (send_sem, recv_sem, pair_send, pair_recv)
        row, self.fsdp = lax.axis_index(AXES[0]), lax.axis_index(AXES[1])
        self.level, self.core = row // 2, row % 2
        self.turn = ring_place(self.fsdp)
        self.rest_rows = rest_flat.shape[0] // 32
        self.row = row

    def spot(self, at_level, at_core, at_turn):
        return (at_level * 2 + at_core, ring_place(at_turn))

    def targets(self):
        right, left = (self.turn + 1) % 4, (self.turn + 3) % 4
        return (
            self.spot(self.level, self.core, right),
            self.spot(self.level, self.core, left),
            self.spot(self.level + 1, self.core, self.turn),
            self.spot(self.level - 1, self.core, self.turn),
            self.spot(self.level, 1 - self.core, self.turn),
        )

    def meet(self):
        barrier = pltpu.get_barrier_semaphore()
        right, left, above, below, sibling = self.targets()

        def tell(target):
            pl.semaphore_signal(barrier, inc=1, device_id=target, device_id_type=MESH)

        for target in (right, left, sibling):
            tell(target)
        pl.when(self.level > 0)(lambda: tell(below))
        pl.when(self.level < 3)(lambda: tell(above))
        inner = (self.level > 0).astype(jnp.int32) + (self.level < 3).astype(jnp.int32)
        pl.semaphore_wait(barrier, 3 + inner)

    def shard_of(self, at_level, at_core, at_turn):
        return (at_level * 2 + at_core) * 4 + ring_place(at_turn)

    def place_own(self, ipa_own, rest_own, mid, mid_send, mid_recv, own_sem):
        me = self.row * 4 + self.fsdp
        odd = self.fsdp % 2
        rest = pltpu.make_async_copy(rest_own, self.rows(REST, me, None), own_sem)
        rest.start()
        other = (self.row, self.fsdp + 1 - 2 * odd)
        copy = pltpu.make_async_remote_copy(
            ipa_own.at[pl.ds(0, 1)], mid, mid_send, mid_recv, device_id=other, device_id_type=MESH
        )
        base = me // 2 * PAIR_ROWS
        flat = self.flats[0]

        @pl.when(odd == 1)
        def _():
            copy.start()
            turned = pltpu.roll(ipa_own[...], LANES // 2, 1)
            low = lax.broadcasted_iota(jnp.int32, (ODD_ROWS, LANES), 1) < LANES // 2
            both = jnp.where(low, turned[0:ODD_ROWS], turned[1 : ODD_ROWS + 1])
            flat[pl.ds(base + EVEN_ROWS, ODD_ROWS), :] = both
            copy.wait_send()

        @pl.when(odd == 0)
        def _():
            flat[pl.ds(base, ODD_ROWS), :] = ipa_own[0:ODD_ROWS, :]
            copy.wait_recv()
            low = lax.broadcasted_iota(jnp.int32, (1, LANES), 1) < LANES // 2
            last = jnp.where(low, ipa_own[ODD_ROWS:EVEN_ROWS, :], pltpu.roll(mid[...], LANES // 2, 1))
            flat[pl.ds(base + ODD_ROWS, 1), :] = last

        rest.wait()

    def rows(self, part, of, odd):
        if part == REST:
            return self.flats[1].at[pl.ds(of * self.rest_rows, self.rest_rows)]
        base = of // 2 * PAIR_ROWS + (EVEN_ROWS if odd else 0)
        first, last = ((0, CUT), (CUT, ODD_ROWS if odd else EVEN_ROWS))[part]
        return self.flats[0].at[pl.ds(base + first, last - first)]

    def on_rows(self, part, of, act):
        if part == REST:
            act(self.rows(part, of, None))
        else:
            pl.when(of % 2 == 0)(lambda: act(self.rows(part, of, False)))
            pl.when(of % 2 == 1)(lambda: act(self.rows(part, of, True)))

    def copy(self, rows, part, of, way):
        send_sem, recv_sem, pair_send, pair_recv = self.sems
        if way == 4:
            send, recv = pair_send.at[part, of], pair_recv.at[part, of]
        else:
            send, recv = send_sem.at[part, of, way], recv_sem.at[part, of]
        return pltpu.make_async_remote_copy(
            rows, rows, send, recv, device_id=self.targets()[way], device_id_type=MESH
        )

    def ways(self, part, up, side, from_level, act):
        if side == 0:
            act(0)
            act(1)
            if up <= 0:
                pl.when(self.level < 3)(lambda: act(2))
            if up >= 0:
                pl.when(self.level > 0)(lambda: act(3))
        elif side == 2:
            if up <= 0 and by_line(part, up - 1):
                pl.when(self.level < 3)(lambda: act(2))
            if up >= 0 and by_line(part, up + 1):
                pl.when(self.level > 0)(lambda: act(3))
        elif not by_line(part, up):
            way = 0 if side == -1 else 1
            pl.when((from_level + part) % 2 == way)(lambda: act(way))
        act(4)

    def when_there(self, up, act):
        from_level = self.level + up
        if up == 0:
            act(from_level)
        else:
            pl.when((from_level >= 0) & (from_level < 4))(lambda: act(from_level))

    def receive(self, part, up, side):
        def act(from_level):
            of = self.shard_of(from_level, self.core, (self.turn + side + 4) % 4)

            def move(rows):
                if (up, side) != (0, 0):
                    self.copy(rows, part, of, 0).wait_recv()
                self.ways(part, up, side, from_level, lambda way: self.copy(rows, part, of, way).start())

            self.on_rows(part, of, move)

        self.when_there(up, act)

    def arrive(self, part, up, side):
        def act(from_level):
            of = self.shard_of(from_level, 1 - self.core, (self.turn + side + 4) % 4)
            self.on_rows(part, of, lambda rows: self.copy(rows, part, of, 4).wait_recv())

        self.when_there(up, act)

    def finish(self, part, up, side):
        def act(from_level):
            of = self.shard_of(from_level, self.core, (self.turn + side + 4) % 4)

            def move(rows):
                self.ways(part, up, side, from_level, lambda way: self.copy(rows, part, of, way).wait_send())

            self.on_rows(part, of, move)

        self.when_there(up, act)


def padded_rows(vector, rows):
    return jnp.pad(vector, (0, rows * LANES - vector.shape[0])).reshape(rows, LANES)


STAGE_ROWS = 512


def matrix_shapes(table):
    return [(name, (rows, up_to(width, LANES))) for name, _, rows, width, _, _ in layout(table)]


def unpack_kernel(ipa_flat, rest_flat, *refs):
    outs, stage = refs[:-1], refs[-1]
    names = [name for table in (ipa_table(), rest_table()) for name, _ in matrix_shapes(table)]
    held = dict(zip(names, outs))
    unpack_into(ipa_flat, layout(ipa_table()), held, stage)
    unpack_into(rest_flat, layout(rest_table()), held, stage)


def unpack_all(ipa_flat, rest_flat):
    shapes = matrix_shapes(ipa_table()) + matrix_shapes(rest_table())
    outs = pl.pallas_call(
        unpack_kernel,
        out_shape=[jax.ShapeDtypeStruct(shape, jnp.float32) for _, shape in shapes],
        in_specs=[pl.BlockSpec(memory_space=pltpu.VMEM)] * 2,
        out_specs=[pl.BlockSpec(memory_space=pltpu.VMEM)] * len(shapes),
        scratch_shapes=[pltpu.VMEM((STAGE_ROWS, LANES), jnp.float32)],
        compiler_params=pltpu.CompilerParams(vmem_limit_bytes=VMEM_LIMIT),
        name="unpack",
    )(ipa_flat, rest_flat)
    return {name: out for (name, _), out in zip(shapes, outs)}


IPA_SLOT = 664
REST_SLOT = 472


PART_ROWS = (CUT, IPA_SLOT - CUT, REST_SLOT)
ROUNDS = (
    (2, 3), (2, 0), (2, 2), (2, 1), (0, 3), (1, 3), (0, 1), (1, 1), (0, 0), (1, 0), (0, 2), (1, 2),
)


class Scatter:
    def __init__(self, ipa_flat, rest_flat, pair_held, half_held, side_held, line_held, sems):
        self.flats = (ipa_flat, rest_flat)
        self.pair_held, self.half_held = pair_held, half_held
        self.side_held, self.line_held = side_held, line_held
        self.sems = sems
        row, self.fsdp = lax.axis_index(AXES[0]), lax.axis_index(AXES[1])
        self.level, self.core = row // 2, row % 2
        turn = ring_place(self.fsdp)
        right, left = (turn + 1) % 4, (turn + 3) % 4
        self.turns = ((turn + 2) % 4, right, left, turn)
        self.sibling = self.spot(self.level, 1 - self.core, turn)
        self.sides = (self.spot(self.level, self.core, right), self.spot(self.level, self.core, left))
        self.lines = (self.spot(self.level + 1, self.core, turn), self.spot(self.level - 1, self.core, turn))

    def spot(self, at_level, at_core, at_turn):
        return (at_level * 2 + at_core, ring_place(at_turn))

    def meet(self):
        barrier = pltpu.get_barrier_semaphore()

        def tell(target):
            pl.semaphore_signal(barrier, inc=1, device_id=target, device_id_type=MESH)

        for target in (self.sibling,) + self.sides:
            tell(target)
        pl.when(self.level < 3)(lambda: tell(self.lines[0]))
        pl.when(self.level > 0)(lambda: tell(self.lines[1]))
        inner = (self.level > 0).astype(jnp.int32) + (self.level < 3).astype(jnp.int32)
        pl.semaphore_wait(barrier, 3 + inner)

    def flat_rows(self, part, at_level, at_core, at_turn):
        of = (at_level * 2 + at_core) * 4 + ring_place(at_turn)
        if part == REST:
            return self.flats[1].at[pl.ds(of * 467, REST_SLOT)]
        return self.flats[0].at[pl.ds((of // 2) * PAIR_ROWS + (of % 2) * ODD_ROWS + part * CUT, PART_ROWS[part])]

    def remote(self, source, target, sems, place, device):
        send, recv = sems
        return pltpu.make_async_remote_copy(
            source, target, send.at[place], recv.at[place], device_id=device, device_id_type=MESH
        )

    def pair_copy(self, part, target, place):
        return self.remote(
            self.flat_rows(part, target, 1 - self.core, self.turns[place]), self.pair_held[part].at[target, place],
            self.sems[0], (part, target, place), self.sibling,
        )

    def half_copy(self, part, target):
        return self.remote(
            self.pair_held[part].at[target, 0], self.half_held[part].at[target],
            self.sems[1], (part, target), self.sides[(target + part) % 2],
        )

    def side_copy(self, part, target, way):
        return self.remote(
            self.pair_held[part].at[target, 1 + way], self.side_held[part].at[target, way],
            self.sems[2], (part, target, way), self.sides[way],
        )

    def line_copy(self, part, target, way, to=None):
        place = 4 if way == 1 and to == target else target
        return self.remote(
            self.pair_held[part].at[target, 3], self.line_held[part].at[place],
            self.sems[3], (part, target, way), self.lines[way],
        )

    def begin(self, turn_of):
        part, target = ROUNDS[turn_of]
        for place in range(4):
            self.pair_copy(part, target, place).start()

    def pair_sum(self, part, target, place):
        self.pair_copy(part, target, place).wait_recv()
        held = self.pair_held[part].at[target, place]
        held[...] = held[...] + self.flat_rows(part, target, self.core, self.turns[place])[...]

    def one(self, turn_of):
        part, target = ROUNDS[turn_of]
        late = (target + part) % 2
        self.pair_sum(part, target, 0)
        self.half_copy(part, target).start()
        self.pair_sum(part, target, 2 - late)
        self.side_copy(part, target, 1 - late).start()
        self.pair_sum(part, target, 1 + late)
        self.pair_sum(part, target, 3)

    def two(self, turn_of):
        part, target = ROUNDS[turn_of]
        late = (target + part) % 2
        self.half_copy(part, target).wait_recv()
        held = self.pair_held[part].at[target, 1 + late]
        held[...] = held[...] + self.half_held[part][target]
        self.side_copy(part, target, late).start()

    def three(self, turn_of):
        part, target = ROUNDS[turn_of]
        self.side_copy(part, target, 0).wait_recv()
        self.side_copy(part, target, 1).wait_recv()
        held = self.pair_held[part].at[target, 3]
        held[...] = held[...] + (self.side_held[part][target, 0] + self.side_held[part][target, 1])
        self.line(turn_of, 0)

    def line(self, turn_of, place):
        part, target = ROUNDS[turn_of]
        for way, level in ((0, place), (1, 3 - place)):
            if (level > target, level < target)[way]:
                continue

            def move(way=way, level=level):
                if place:
                    self.line_copy(part, target, way, level).wait_recv()
                    held = self.pair_held[part].at[target, 3]
                    held[...] = held[...] + self.line_held[part][4 if way == 1 and level == target else target]
                if level != target:
                    self.line_copy(part, target, way, level + 1 - 2 * way).start()

            if place or level != target:
                pl.when(self.level == level)(move)

    def finish(self, ipa_out, rest_out):
        own = jnp.concatenate([self.pair_held[part][self.level, 3] for part in (0, 1)], 0)
        whole = pltpu.roll(own, LANES // 2, 1)
        after = jnp.concatenate([whole[1:], whole[:1]], 0)
        low = lax.broadcasted_iota(jnp.int32, own.shape, 1) < LANES // 2
        ipa_out[...] = jnp.where(self.fsdp % 2 == 1, jnp.where(low, whole, after), own)
        rest_out[...] = self.pair_held[REST][self.level, 3][:467]
        for part, target in ROUNDS:
            for place in range(4):
                self.pair_copy(part, target, place).wait_send()
            self.half_copy(part, target).wait_send()
            for way in (0, 1):
                self.side_copy(part, target, way).wait_send()
            if target > 0:
                pl.when(self.level < target)(lambda: self.line_copy(part, target, 0).wait_send())
            if target < 3:
                pl.when(self.level > target)(lambda: self.line_copy(part, target, 1).wait_send())


def scatter_scratch():
    slots = [(rows, LANES) for rows in PART_ROWS]
    shapes = [lead + slot for lead in ((4, 4), (4,), (4, 2), (5,)) for slot in slots]
    counts = [(3, 4, 4), (3, 4), (3, 4, 2), (3, 4, 2)]
    buffers = [pltpu.VMEM(shape, jnp.float32) for shape in shapes]
    return buffers + [pltpu.SemaphoreType.DMA(count) for count in counts for _ in range(2)]


def scatter_of(ipa_flat, rest_flat, scratch):
    held = [tuple(scratch[k : k + 3]) for k in range(0, 12, 3)]
    sems = [tuple(scratch[k : k + 2]) for k in range(12, 20, 2)]
    return Scatter(ipa_flat, rest_flat, *held, sems)


IPA_ROWS = 21144
REST_ROWS = 14952
IPA_ORDER = list(ipa_table())
TIME_NAME, OUT_NAME, HEAD_NAMES = IPA_ORDER[0], IPA_ORDER[18], IPA_ORDER[3:9]


def clear_tail(flat, table):
    _, offset, rows, width, _, _ = layout(table)[-1]
    full = (offset + rows * width) // LANES
    flat[full:, :] = jnp.zeros((flat.shape[0] - full, LANES), jnp.float32)


def store_lines(flat, row, lane, stride, tile):
    count = tile.shape[0]
    here = row_slice(row, count, stride)
    if lane == 0:
        flat[here, :] = tile
        return
    turned = pltpu.roll(tile, lane, 1)
    at = lax.broadcasted_iota(jnp.int32, tile.shape, 1)
    flat[here, :] = jnp.where(at >= lane, turned, flat[here, :])
    after = row_slice(row + 1, count, stride)
    flat[after, :] = jnp.where(at < lane, turned, flat[after, :])


def gather_any(ipa_params, rest_params):
    flats = []
    for shard in (ipa_params, rest_params):
        full = lax.all_gather(shard, AXES, axis=0, tiled=True)
        flats.append(full.reshape(-1, LANES))
    return flats


def scatter_any(ipa_flat, rest_flat, ipa_params, rest_params):
    owned = []
    for flat, shard in ((ipa_flat, ipa_params), (rest_flat, rest_params)):
        own = shard.shape[0]
        count = lax.axis_size(AXES[0]) * lax.axis_size(AXES[1])
        cut = flat.reshape(-1)[: own * count].reshape(count, own)
        owned.append(lax.psum_scatter(cut, AXES, scatter_dimension=0, tiled=True).reshape(-1))
    return owned


def small_slice(ipa_params, rest_params):
    whole = (lax.axis_size(AXES[0]), lax.axis_size(AXES[1])) == (8, 4)
    return whole and ipa_params.shape[0] == 84544 and rest_params.shape[0] == 59776


def split(value):
    high = value.astype(jnp.bfloat16)
    return high, (value - high.astype(jnp.float32)).astype(jnp.bfloat16)


def dot_one(left, right, dims=((1,), (0,))):
    return lax.dot_general(left, right, (dims, ((), ())), preferred_element_type=jnp.float32)


def beside(pair):
    high, low = pair
    return jnp.concatenate([high, high, low], 1)


def above(pair):
    high, low = pair
    return jnp.concatenate([high, low, high], 0)


def dot_rows(left, right):
    dims = ((0,), (0,))
    return (
        dot_one(left[0], right[0], dims) + dot_one(left[0], right[1], dims) + dot_one(left[1], right[0], dims)
    )


def dot_high(left, right, dims=((1,), (0,))):
    return lax.dot_general(
        left, right, (dims, ((), ())), precision=lax.Precision.HIGH, preferred_element_type=jnp.float32
    )


NT = ((1,), (1,))
TN = ((0,), (0,))
GELU_IN = math.sqrt(2.0 / math.pi)
GELU_CUBE = 0.044715


def gelu_both(value):
    square = value * value
    bent = jnp.tanh(value * (GELU_IN + (GELU_IN * GELU_CUBE) * square))
    half = 0.5 + 0.5 * bent
    slope = half + (0.5 * value) * (1.0 - bent * bent) * (GELU_IN + (3.0 * GELU_IN * GELU_CUBE) * square)
    return value * half, slope


def norm_both(value):
    count = value.shape[-1]
    centered = value - jnp.sum(value, -1, keepdims=True) * (1.0 / count)
    spread = jnp.sum(centered * centered, -1, keepdims=True) * (1.0 / count)
    inverse = lax.rsqrt(spread + 1e-05)
    return centered * inverse, inverse


def norm_back(cot, unit, inverse):
    count = cot.shape[-1]
    mean = jnp.sum(cot, -1, keepdims=True) * (1.0 / count)
    along = jnp.sum(cot * unit, -1, keepdims=True) * (1.0 / count)
    return inverse * (cot - mean - unit * along)


EDGE_ROWS = 512
EDGE_CHAINS = 2


def edge_kernel(
    edge, cot, proj, node, turned, moved, one_w, one_b, two_w, two_b, final_w, final_b, gain, shift,
    node_out, turned_out, moved_out, out, edge_grad, proj_grad, one_gw, one_gb, two_gw, two_gb, final_gw, final_gb, gain_g, shift_g,
    one_in, two_in, final_in, one_back, two_back, final_back, one_i, one_j, final_i, final_j,
    sum_one_i, sum_one_j, sum_final_i, sum_final_j,
):
    step = pl.program_id(0)
    own = EDGE_ROWS // 32
    length = 32

    @pl.when(step == 0)
    def _():
        node_out[...] = node[...]
        turned_out[...] = turned[...]
        moved_out[...] = moved[...]
        first = one_w[0:E, :]
        one_in[...] = above(split(first))
        one_back[...] = above(split(first.T))
        two_in[...] = above(split(two_w[...]))
        two_back[...] = above(split(two_w[...].T))
        final_in[...] = above(split(final_w[...]))
        final_back[...] = above(split(final_w[...].T))
        held = proj[...]
        one_i[...] = dot_high(held, one_w[E : 2 * E, :]) + one_b[...]
        one_j[...] = dot_high(held, one_w[2 * E :, :])
        final_i[...] = dot_high(held, final_w[E : 2 * E, :]) + final_b[...]
        final_j[...] = dot_high(held, final_w[2 * E :, :])
        for ref in (
            one_gw, one_gb, two_gw, two_gb, final_gw, final_gb, gain_g, shift_g,
            sum_one_j, sum_final_j,
        ):
            ref[...] = jnp.zeros_like(ref)

    half = EDGE_ROWS // EDGE_CHAINS
    crop = pl.ds(pl.multiple_of(step // (length // own) * length, length), length)

    def chain(place):
        rows = pl.ds(place * half, half)
        few = half // length
        here = pl.ds(pl.multiple_of(step * own + place * few, few), few)

        def spread(own_rows, other_rows):
            return (own_rows[:, None, :] + other_rows[None, :, :]).reshape(half, -1)

        def sums(value):
            cube = value.reshape(few, length, -1)
            return jnp.sum(cube, 1), jnp.sum(cube, 0)

        edges = edge[rows, :]
        edge_pair = split(edges)
        first = dot_one(beside(edge_pair), one_in[...])
        yield
        one_act, one_slope = gelu_both(first + spread(one_i[here, :], one_j[crop, :]))
        one_pair = split(one_act)
        yield
        second = dot_one(beside(one_pair), two_in[...])
        yield
        two_act, two_slope = gelu_both(second + two_b[...])
        mixed = jnp.concatenate([two_act[:, :E] + edges, two_act[:, E:]], 1)
        mixed_pair = split(mixed)
        yield
        result = dot_one(beside(mixed_pair), final_in[...])
        yield
        unit, inverse = norm_both(result + spread(final_i[here, :], final_j[crop, :]))
        out[rows, :] = unit * gain[...] + shift[...]
        cots = cot[rows, :]
        gain_g[...] += jnp.sum(cots * unit, 0, keepdims=True)
        shift_g[...] += jnp.sum(cots, 0, keepdims=True)
        result_c = norm_back(cots * gain[...], unit, inverse)
        result_pair = split(result_c)
        yield
        mixed_c = dot_one(beside(result_pair), final_back[...])
        final_gw[...] += dot_rows(mixed_pair, result_pair)
        yield
        edge_grad[rows, :] = mixed_c[:, :E]
        two_c = mixed_c * two_slope
        two_pair = split(two_c)
        two_gb[...] += jnp.sum(two_c, 0, keepdims=True)
        over_j, over_i = sums(result_c)
        sum_final_i[here, :] = over_j
        sum_final_j[crop, :] += over_i
        yield
        one_c = dot_one(beside(two_pair), two_back[...])
        two_gw[...] += dot_rows(one_pair, two_pair)
        yield
        one_c = one_c * one_slope
        one_back_pair = split(one_c)
        over_j, over_i = sums(one_c)
        sum_one_i[here, :] = over_j
        sum_one_j[crop, :] += over_i
        yield
        edge_grad[rows, :] = edge_grad[rows, :] + dot_one(beside(one_back_pair), one_back[...])
        one_gw[0:E, :] += dot_rows(edge_pair, one_back_pair)
        yield

    chains = [chain(place) for place in range(EDGE_CHAINS)]
    for beat in range(11 + EDGE_CHAINS - 1):
        for place, flow in enumerate(chains):
            if 0 <= beat - place < 11:
                next(flow)

    @pl.when(step == pl.num_programs(0) - 1)
    def _():
        held = proj[...]
        one_gb[...] = jnp.sum(sum_one_i[...], 0, keepdims=True)
        final_gb[...] = jnp.sum(sum_final_i[...], 0, keepdims=True)
        one_gw[E : 2 * E, :] = dot_high(held, sum_one_i[...], TN)
        one_gw[2 * E :, :] = dot_high(held, sum_one_j[...], TN)
        final_gw[E : 2 * E, :] += dot_high(held, sum_final_i[...], TN)
        final_gw[2 * E :, :] += dot_high(held, sum_final_j[...], TN)
        proj_grad[...] = (
            dot_high(sum_one_i[...], one_w[E : 2 * E, :], NT)
            + dot_high(sum_one_j[...], one_w[2 * E :, :], NT)
            + dot_high(sum_final_i[...], final_w[E : 2 * E, :], NT)
            + dot_high(sum_final_j[...], final_w[2 * E :, :], NT)
        )


def edge_all(edge, cot, proj, passed, mats):
    rows, nodes = edge.shape[0], proj.shape[0]
    params = [mats[name] for name in EDGE_NAMES]
    by_step = pl.BlockSpec((EDGE_ROWS, E), lambda step: (step, 0))

    def whole(array):
        return pl.BlockSpec(array.shape, lambda step: (0,) * array.ndim)

    def like(array):
        return jax.ShapeDtypeStruct(array.shape, jnp.float32)

    def held(dtype, *shape):
        return pltpu.VMEM(shape, dtype)

    wide = 3 * E
    bf16, f32 = jnp.bfloat16, jnp.float32
    outs = pl.pallas_call(
        edge_kernel,
        grid=(rows // EDGE_ROWS,),
        out_shape=[like(array) for array in (*passed, edge, edge, proj)] + [like(array) for array in params],
        in_specs=[by_step, by_step, whole(proj)] + [whole(array) for array in (*passed, *params)],
        out_specs=[whole(array) for array in passed] + [by_step, by_step, whole(proj)] + [whole(array) for array in params],
        scratch_shapes=[
            held(bf16, 3 * E, wide), held(bf16, 3 * wide, wide), held(bf16, 3 * wide, E),
            held(bf16, 3 * wide, E), held(bf16, 3 * wide, wide), held(bf16, 3 * E, wide),
            held(f32, nodes, wide), held(f32, nodes, wide), held(f32, nodes, E), held(f32, nodes, E),
            held(f32, nodes, wide), held(f32, nodes, wide), held(f32, nodes, E), held(f32, nodes, E),
        ],
        compiler_params=pltpu.CompilerParams(vmem_limit_bytes=VMEM_LIMIT),
        name="edge_update",
    )(edge, cot, proj, *passed, *params)
    return outs[:6], dict(zip(EDGE_NAMES, outs[6:]))


THIRD = math.sqrt(1.0 / 3.0)
POINT_SCALE = math.sqrt(2.0 / (9.0 * QPTS)) / 2.0
HIDDEN_LOGIT = -1000000000.0
Q_AXIS, V_AXIS = HEADS * QPTS, HEADS * VPTS
SCALAR_OUT = HEADS * HEAD_DIM
POINT_ROWS = 4 * V_AXIS
GROUP = 8


def iota(shape, axis):
    return lax.broadcasted_iota(jnp.int32, shape, axis)


def ones_where(condition):
    return jnp.where(condition, 1.0, 0.0)


def dot_marks(value, marks, dims=((1,), (0,))):
    high, low = split(value)
    marks = marks.astype(jnp.bfloat16)
    return dot_one(high, marks, dims) + dot_one(low, marks, dims)


def rows_of(ref):
    return jnp.concatenate([ref[:, crop, :] for crop in range(ref.shape[1])], 1)


def put_rows(ref, rows):
    for crop in range(ref.shape[1]):
        ref[:, crop, :] = rows[:, crop * 32 : (crop + 1) * 32]


def rotation_rows(one, two, three):
    norm = lax.rsqrt(1.0 + (one * one + two * two + three * three))
    b, c, d = one * norm, two * norm, three * norm
    a = norm
    return [
        a * a + b * b - c * c - d * d,
        2.0 * (b * c - a * d),
        2.0 * (b * d + a * c),
        2.0 * (b * c + a * d),
        a * a - b * b + c * c - d * d,
        2.0 * (c * d - a * b),
        2.0 * (b * d - a * c),
        2.0 * (c * d + a * b),
        a * a - b * b - c * c + d * d,
    ]


def frame_rows(turn, move, update):
    own = rotation_rows(*turn)
    new = rotation_rows(*update[:3])
    turned = [
        own[3 * c] * new[e] + own[3 * c + 1] * new[3 + e] + own[3 * c + 2] * new[6 + e]
        for c in range(3)
        for e in range(3)
    ]
    moved = [
        own[3 * c] * update[3] + own[3 * c + 1] * update[4] + own[3 * c + 2] * update[5] + move[c]
        for c in range(3)
    ]
    return turned, moved


def single_rows(block, count):
    return [block[k : k + 1, :] for k in range(count)]


def turned_over(rows):
    count = rows[0].shape[1]
    held = jnp.concatenate(rows + [jnp.zeros((count - len(rows), count), jnp.float32)], 0)
    return held.T


def axis_parts(value, size):
    return [value[:, k * size : (k + 1) * size] for k in range(3)]


def to_global_points(flat, size, turn, move):
    local = axis_parts(flat, size)
    out = [
        turn[3 * c] * local[0] + turn[3 * c + 1] * local[1] + turn[3 * c + 2] * local[2] + move[c]
        for c in range(3)
    ]
    return jnp.concatenate(out, 1)


def softmax_rows(logits):
    raised = jnp.exp(logits - jnp.max(logits, -1, keepdims=True))
    return raised / jnp.sum(raised, -1, keepdims=True)


def softmax_back(cot, weights):
    return weights * (cot - jnp.sum(cot * weights, -1, keepdims=True))


def lane_pick(row, place):
    return jnp.sum(jnp.where(iota(row.shape, 1) == place, row, 0.0), -1, keepdims=True)


def softplus(value):
    return jnp.maximum(value, 0.0) + jnp.log(1.0 + jnp.exp(-jnp.abs(value)))


def head_lanes(shape, size, head, span=None):
    lane = iota(shape, 1)
    if span is not None:
        lane = lane % span
    return ones_where(lane // size == head)


def group_mask():
    shape = (GROUP * HEADS, GROUP * 32)
    return ones_where(iota(shape, 0) // HEADS == iota(shape, 1) // 32)


def group_fold(count):
    shape = (GROUP * 32, count)
    return ones_where(iota(shape, 0) % 32 == iota(shape, 1) % 32)


class Block(NamedTuple):
    in_w: Any
    in_b: Any
    out_w: Any
    out_b: Any
    first_gain: Any
    first_shift: Any
    one_w: Any
    one_b: Any
    two_w: Any
    two_b: Any
    second_gain: Any
    second_shift: Any


class BlockSlots(NamedTuple):
    x: int
    q: int
    k: int
    v: int
    mix: int
    unit: int
    act: int
    slope: int
    last: int


class NodeSlots(NamedTuple):
    x: int
    mid: int
    act_a: int
    slope_a: int
    act_b: int
    slope_b: int
    tail: int
    inverse: int


class PointSlots(NamedTuple):
    time: int
    unit: int
    pg: int
    feats: int
    gq: int
    gk: int
    gv: int
    inverse: int


BLOCK_SLOTS = [BlockSlots(*range(9 * tag, 9 * tag + 9)) for tag in (0, 1)]
NODE_SLOTS = NodeSlots(*range(18, 26))
POINT_SLOTS = PointSlots(*range(8))
SLOTS = 26
KEPT_WIDTH = 384
SIZE = WIDTH // TF_HEADS


def named(table, refs):
    return SimpleNamespace(**dict(zip(table, refs)))


def block_of(refs, tag):
    return Block(*refs[2 + 12 * tag : 14 + 12 * tag])


def keeper(kept):
    def keep(slot, value):
        kept[slot, :, 0 : value.shape[1]] = value

    return keep


def vector(ref, width=WIDTH):
    return ref[:, :width]


def encoder_forward(block, tag, hidden, same, kept, probs):
    slots, keep = BLOCK_SLOTS[tag], keeper(kept)
    keep(slots.x, hidden)
    packed = dot_high(hidden, block.in_w[...]) + block.in_b[...]
    query, key, value = (packed[:, k * WIDTH : (k + 1) * WIDTH] for k in range(3))
    keep(slots.q, query)
    keep(slots.k, key)
    keep(slots.v, value)
    mixed = jnp.zeros_like(query)
    for head in range(TF_HEADS):
        mask = head_lanes(query.shape, SIZE, head)
        scores = dot_high(query * mask, key, NT) * SIZE ** (-0.5)
        weights = softmax_rows(jnp.where(same, scores, HIDDEN_LOGIT))
        probs[tag * TF_HEADS + head] = weights
        mixed = mixed + dot_high(weights, value * mask)
    keep(slots.mix, mixed)
    attended = dot_high(mixed, block.out_w[:, :WIDTH]) + vector(block.out_b)
    unit, first_inverse = norm_both(hidden + attended)
    keep(slots.unit, unit)
    normed = unit * vector(block.first_gain) + vector(block.first_shift)
    act, slope = gelu_both(dot_high(normed, block.one_w[:, :WIDTH]) + vector(block.one_b))
    keep(slots.act, act)
    keep(slots.slope, slope)
    feed = dot_high(act, block.two_w[:, :WIDTH]) + vector(block.two_b)
    last, second_inverse = norm_both(normed + feed)
    keep(slots.last, last)
    return last * vector(block.second_gain) + vector(block.second_shift), [first_inverse, second_inverse]


def linear_back(weight, weight_grad, bias_grad, value, cot):
    width = cot.shape[1]
    weight_grad[:, :width] = dot_high(value, cot, TN)
    bias_grad[:, :width] = jnp.sum(cot, 0, keepdims=True)
    return dot_high(cot, weight[:, :width], NT)


def affine_back(gain, gain_grad, shift_grad, unit, cot):
    width = cot.shape[1]
    gain_grad[:, :width] = jnp.sum(cot * unit, 0, keepdims=True)
    shift_grad[:, :width] = jnp.sum(cot, 0, keepdims=True)
    return cot * gain[:, :width]


def encoder_back(block, grads, tag, cot, kept, probs, inverses):
    slots = BLOCK_SLOTS[tag]
    held = lambda slot: kept[slot, :, 0:WIDTH]
    first_inverse, second_inverse = inverses
    last, unit = held(slots.last), held(slots.unit)
    cot = affine_back(block.second_gain, grads.second_gain, grads.second_shift, last, cot)
    summed = norm_back(cot, last, second_inverse)
    inner = linear_back(block.two_w, grads.two_w, grads.two_b, held(slots.act), summed) * held(slots.slope)
    normed = unit * vector(block.first_gain) + vector(block.first_shift)
    normed_c = summed + linear_back(block.one_w, grads.one_w, grads.one_b, normed, inner)
    normed_c = affine_back(block.first_gain, grads.first_gain, grads.first_shift, unit, normed_c)
    hidden_c = norm_back(normed_c, unit, first_inverse)
    mixed_c = linear_back(block.out_w, grads.out_w, grads.out_b, held(slots.mix), hidden_c)
    query, key, value = held(slots.q), held(slots.k), held(slots.v)
    query_c, key_c, value_c = (jnp.zeros_like(query) for _ in range(3))
    for head in range(TF_HEADS):
        mask = head_lanes(query.shape, SIZE, head)
        weights = probs[tag * TF_HEADS + head]
        scores_c = softmax_back(dot_high(mixed_c * mask, value, NT), weights) * SIZE ** (-0.5)
        value_c = value_c + dot_high(weights, mixed_c * mask, TN)
        query_c = query_c + dot_high(scores_c, key * mask)
        key_c = key_c + dot_high(scores_c, query * mask, TN)
    packed_c = jnp.concatenate([query_c, key_c, value_c], 1)
    return hidden_c + linear_back(block.in_w, grads.in_w, grads.in_b, held(slots.x), packed_c)


UNROLL = 4


def each_group(first, last, body):
    several = UNROLL if (last - first) % UNROLL == 0 else 1

    def some(turn_of, _):
        for k in range(several):
            body(first + turn_of * several + k)
        return 0

    lax.fori_loop(0, (last - first) // several, some, 0)


def head_rows(head, count):
    return pl.ds(head, count, stride=HEADS)


def forward_body(ins, ipa, rest, rest_refs, outs, scratch, before_ipa, beside_head, before_rest):
    node_ref, time_ref, turn_ref, move_ref, chain_ref, edge_ref = ins
    node_out, proj_out, rot_out, trans_out, kept, probs, kept_points, wide, attend, pair_held = outs
    att, points, key_squares = scratch
    slots, keep = NODE_SLOTS, keeper(kept)
    point_slots, keep_point = POINT_SLOTS, keeper(kept_points)
    count = node_ref.shape[0]
    square = (count, count)

    turn_rows, move_rows = rows_of(turn_ref), rows_of(move_ref)
    code = jnp.concatenate([chain_ref[crop : crop + 1, :] + 8 * crop for crop in range(chain_ref.shape[0])], 1)
    code = code.astype(jnp.float32)
    turn, move = single_rows(turn_rows, 3), single_rows(move_rows, 3)
    columns = turned_over(rotation_rows(*turn) + move + [code])
    column = [columns[:, k : k + 1] for k in range(13)]
    turn_c, move_c = column[:9], column[9:12]
    same = column[12] == code

    before_ipa()
    node = node_ref[...]
    node_time = node + dot_high(time_ref[...], ipa.time_w[...])
    keep_point(point_slots.time, node_time)

    pair_turned = jnp.concatenate([ipa.pair_w[...]], 0).T[0:HEADS, :]
    group = group_mask()
    fold = group_fold(count)

    def pair_rows(place):
        at = pl.multiple_of(place * GROUP * 32, GROUP * 32)
        edges = edge_ref[pl.ds(at, GROUP * 32), :]
        biased = dot_high(pair_turned, edges, NT)
        tiled = jnp.concatenate([biased] * GROUP, 0) * group
        here = pl.ds(pl.multiple_of(place * GROUP * HEADS, GROUP * HEADS), GROUP * HEADS)
        pair_held[here, :] = dot_marks(tiled, fold)

    each_group(0, count // GROUP, pair_rows)

    def point_set(weight, bias, size):
        flat = dot_high(node_time, weight[:, : 3 * size]) + bias[:, : 3 * size]
        return to_global_points(flat, size, turn_c, move_c)

    query_pts = point_set(ipa.qpoint_w, ipa.qpoint_b, Q_AXIS)
    key_pts = point_set(ipa.kpoint_w, ipa.kpoint_b, Q_AXIS)
    value_pts = point_set(ipa.vpoint_w, ipa.vpoint_b, V_AXIS)
    keep_point(point_slots.gq, query_pts)
    keep_point(point_slots.gk, key_pts)
    keep_point(point_slots.gv, value_pts)
    key_marks = ones_where((iota((16, 3 * Q_AXIS), 1) % Q_AXIS) // QPTS == iota((16, 3 * Q_AXIS), 0))
    key_squares[...] = dot_high(key_marks, key_pts * key_pts, NT)
    query_squares = query_pts * query_pts
    att[...] = jnp.zeros_like(att)
    points[...] = jnp.zeros_like(points)
    point_weights = softplus(ipa.head_w[...]) * POINT_SCALE
    pair_shift = ipa.pair_b[...]

    def one_head(head, _):
        beside_head(head)
        cols = pl.ds(pl.multiple_of(head * HEAD_DIM, HEAD_DIM), HEAD_DIM)
        query = dot_high(node_time, ipa.query_w[:, cols]) + ipa.query_b[:, cols]
        key = dot_high(node_time, ipa.key_w[:, cols]) + ipa.key_b[:, cols]
        value = dot_high(node_time, ipa.value_w[:, cols]) + ipa.value_b[:, cols]
        wide[0, :, cols] = query
        wide[1, :, cols] = key
        wide[2, :, cols] = value
        mask = head_lanes(query_pts.shape, QPTS, head, Q_AXIS)
        cross = dot_high(query_pts * mask, key_pts, NT)
        own_square = jnp.sum(query_squares * mask, -1, keepdims=True)
        distance = own_square + key_squares[pl.ds(head, 1), :] - 2.0 * cross
        logits = dot_high(query, key, NT) * HEAD_DIM ** (-0.5) + pair_held[head_rows(head, count), :]
        logits = logits + lane_pick(pair_shift, head) - lane_pick(point_weights, head) * distance
        weights = softmax_rows(jnp.where(same, THIRD * logits, HIDDEN_LOGIT))
        attend[head_rows(head, count), :] = weights
        mixed = dot_high(weights, value)
        wide[3, :, cols] = mixed
        att[...] = att[...] + dot_high(mixed, ipa.out_w[cols, :])
        points[...] = points[...] + dot_high(
            weights, value_pts * head_lanes(value_pts.shape, VPTS, head, V_AXIS)
        )
        return 0

    lax.fori_loop(0, HEADS, one_head, 0)

    global_out = axis_parts(points[...], V_AXIS)
    shifted = [global_out[d] - move_c[d] for d in range(3)]
    local = [turn_c[c] * shifted[0] + turn_c[3 + c] * shifted[1] + turn_c[6 + c] * shifted[2] for c in range(3)]
    norm = jnp.sqrt((local[0] * local[0] + local[1] * local[1] + local[2] * local[2]) + 1.0)
    feats = jnp.concatenate(local + [norm], 1)
    keep_point(point_slots.pg, jnp.concatenate(shifted, 1))
    keep_point(point_slots.feats, feats)
    att[...] = att[...] + dot_high(feats, ipa.out_w[SCALAR_OUT : SCALAR_OUT + POINT_ROWS, :])

    def pair_sums(place):
        at = pl.multiple_of(place * GROUP * 32, GROUP * 32)
        here = pl.ds(pl.multiple_of(place * GROUP * HEADS, GROUP * HEADS), GROUP * HEADS)
        spread = dot_marks(attend[here, :], fold, NT) * group
        pair_held[here, :] = dot_high(spread, edge_ref[pl.ds(at, GROUP * 32), :])

    each_group(0, count // GROUP, pair_sums)

    def pair_out(head, _):
        rows = pl.ds(pl.multiple_of(SCALAR_OUT + POINT_ROWS + head * E, E), E)
        att[...] = att[...] + dot_high(pair_held[head_rows(head, count), :], ipa.out_w[rows, :])
        return 0

    lax.fori_loop(0, HEADS, pair_out, 0)

    ipa_unit, ipa_inverse = norm_both(node_time + (att[...] + ipa.out_b[...]))
    keep_point(point_slots.unit, ipa_unit)
    node_ipa = ipa_unit * ipa.ipa_gain[...] + ipa.ipa_shift[...]
    before_rest()
    skipped = (dot_high(node, rest.skip_w[...]) + rest.skip_b[...])[:, :SKIP]
    hidden = jnp.concatenate([node_ipa, skipped], 1)
    hidden, first = encoder_forward(block_of(rest_refs, 0), 0, hidden, same, kept, probs)
    hidden, second = encoder_forward(block_of(rest_refs, 1), 1, hidden, same, kept, probs)
    keep(slots.x, hidden)
    node_mid = node_ipa + dot_high(hidden, rest.post_w[...]) + rest.post_b[...]
    keep(slots.mid, node_mid)
    act_a, slope_a = gelu_both(dot_high(node_mid, rest.trans_one_w[...]) + rest.trans_one_b[...])
    act_b, slope_b = gelu_both(dot_high(act_a, rest.trans_two_w[...]) + rest.trans_two_b[...])
    keep(slots.act_a, act_a)
    keep(slots.slope_a, slope_a)
    keep(slots.act_b, act_b)
    keep(slots.slope_b, slope_b)
    feed = dot_high(act_b, rest.trans_three_w[...]) + rest.trans_three_b[...]
    tail, tail_inverse = norm_both(node_mid + feed)
    keep(slots.tail, tail)
    done = tail * rest.trans_gain[...] + rest.trans_shift[...]
    node_out[...] = done
    proj_out[...] = dot_high(done, rest.edge_node_w[...]) + rest.edge_node_b[...]
    inverses = first + second + [tail_inverse]
    keep_point(point_slots.inverse, jnp.broadcast_to(ipa_inverse, square))
    lane = iota(square, 1)
    kept[slots.inverse, :, 0:count] = sum(jnp.where(lane == k, inverse, 0.0) for k, inverse in enumerate(inverses))
    update = dot_high(done, rest.backbone_w[...]) + rest.backbone_b[...]
    update_rows = single_rows(update.T, 6)
    turned, moved = frame_rows(turn, move, update_rows)
    put_rows(rot_out, jnp.concatenate(turned, 0))
    put_rows(trans_out, jnp.concatenate(moved, 0))


def plain_forward_kernel(*refs):
    names = list(rest_table())[:-8]
    ipa_refs, rest_refs = refs[6:26], refs[26 : 26 + len(names)]
    after = refs[26 + len(names) :]
    nothing = lambda *_: None
    ipa, rest = named(ipa_table(), ipa_refs), named(names, rest_refs)
    forward_body(refs[:6], ipa, rest, rest_refs, after[:10], after[10:], nothing, nothing, nothing)


def forward_kernel(*refs):
    ipa_names, rest_names = list(ipa_table()), list(rest_table())
    many = len(ipa_names) + len(rest_names)
    ipa_own, rest_own = refs[:2]
    outs, mats_out = refs[8:18], refs[18 : 18 + many]
    mats = refs[18 + many : 18 + 2 * many]
    (
        att, points, key_squares, ipa_flat, rest_flat, stage, mid,
        send, recv, pair_send, pair_recv, mid_send, mid_recv, own_sem, mat_sem,
    ) = refs[18 + 2 * many :]
    ipa_refs, rest_refs = mats[: len(ipa_names)], mats[len(ipa_names) :]
    gather = Gather(ipa_flat, rest_flat, send, recv, pair_send, pair_recv)
    entries = hops()
    last = max(place for place, entry in enumerate(entries) if entry[0] != REST)
    left = entries[last + 1 :]

    def mat_copies(first, refs_of):
        return [
            pltpu.make_async_copy(ref, mats_out[first + k], mat_sem.at[first + k]) for k, ref in enumerate(refs_of)
        ]

    def before_ipa():
        gather.meet()
        gather.place_own(ipa_own, rest_own, mid, mid_send, mid_recv, own_sem)
        for entry in entries[: last + 1]:
            gather.receive(*entry)
        for entry in entries:
            if entry[0] != REST:
                gather.arrive(*entry)
        unpack_into(ipa_flat, layout(ipa_table()), dict(zip(ipa_names, ipa_refs)), stage)
        for copy in mat_copies(0, ipa_refs):
            copy.start()

    def beside_head(head):
        for k in range(HEADS):
            now = left[k * len(left) // HEADS : (k + 1) * len(left) // HEADS]

            def receive(now=now):
                for entry in now:
                    gather.receive(*entry)

            if now:
                pl.when(head == k)(receive)

    def before_rest():
        for entry in entries:
            if entry[0] == REST:
                gather.arrive(*entry)
        unpack_into(rest_flat, layout(rest_table()), dict(zip(rest_names, rest_refs)), stage)
        for copy in mat_copies(len(ipa_names), rest_refs):
            copy.start()

    ipa, rest = named(ipa_names, ipa_refs), named(rest_names, rest_refs)
    forward_body(
        refs[2:8], ipa, rest, rest_refs, outs, (att, points, key_squares), before_ipa, beside_head, before_rest
    )
    for entry in entries:
        gather.finish(*entry)
    for copy in mat_copies(0, mats):
        copy.wait()


def rest_backward_kernel(*refs):
    node_cot, proj_cot, rot_cot, trans_cot, node_ref, turn_ref, move_ref, kept, probs = refs[:9]
    names = list(rest_table())
    many = len(names)
    rest_refs, edge_grads = refs[9 : 1 + many], refs[1 + many : 9 + many]
    ipa_out, skip_out, frame_out, flat = refs[9 + many : 13 + many]
    rest_out, stage = refs[13 + many : -1], refs[-1]
    rest, rest_g = named(names[:-8], rest_refs), named(names[:-8], rest_out)
    slots = NODE_SLOTS
    held = lambda slot, width=D: kept[slot, :, 0:width]

    turn, move = single_rows(rows_of(turn_ref), 3), single_rows(rows_of(move_ref), 3)
    inverse = [kept[slots.inverse, :, k : k + 1] for k in range(5)]

    tail = held(slots.tail)
    done = tail * rest.trans_gain[...] + rest.trans_shift[...]
    update = dot_high(done, rest.backbone_w[...]) + rest.backbone_b[...]
    _, frame_pull = jax.vjp(frame_rows, turn, move, single_rows(update.T, 6))
    turn_first, move_first, update_rows = frame_pull(
        (single_rows(rows_of(rot_cot), 9), single_rows(rows_of(trans_cot), 3))
    )
    update_c = turned_over(update_rows)
    done_c = node_cot[...] + linear_back(rest.backbone_w, rest_g.backbone_w, rest_g.backbone_b, done, update_c)
    done_c = done_c + linear_back(
        rest.edge_node_w, rest_g.edge_node_w, rest_g.edge_node_b, done, proj_cot[...]
    )
    done_c = affine_back(rest.trans_gain, rest_g.trans_gain, rest_g.trans_shift, tail, done_c)
    mid_c = norm_back(done_c, tail, inverse[4])
    flow = linear_back(
        rest.trans_three_w, rest_g.trans_three_w, rest_g.trans_three_b, held(slots.act_b), mid_c
    ) * held(slots.slope_b)
    flow = linear_back(
        rest.trans_two_w, rest_g.trans_two_w, rest_g.trans_two_b, held(slots.act_a), flow
    ) * held(slots.slope_a)
    mid_c = mid_c + linear_back(
        rest.trans_one_w, rest_g.trans_one_w, rest_g.trans_one_b, held(slots.mid), flow
    )
    hidden_c = linear_back(rest.post_w, rest_g.post_w, rest_g.post_b, held(slots.x, WIDTH), mid_c)
    for tag in (1, 0):
        hidden_c = encoder_back(
            block_of(rest_refs, tag), block_of(rest_out, tag), tag, hidden_c, kept, probs,
            inverse[2 * tag : 2 + 2 * tag],
        )
    ipa_out[...] = mid_c + hidden_c[:, :D]
    skip_out[...] = linear_back(rest.skip_w, rest_g.skip_w, rest_g.skip_b, node_ref[...], hidden_c[:, D:])

    frame_out[...] = jnp.concatenate(list(turn_first) + list(move_first) + [jnp.zeros_like(turn[0])] * 2, 0)
    clear_tail(flat, rest_table())
    pack_into(flat, layout(rest_table()), dict(zip(names, rest_out + edge_grads)), stage)


POINT_AT = SCALAR_OUT
POINT_NAMES = (IPA_ORDER[9], IPA_ORDER[11], IPA_ORDER[13])
SMALL_NAMES = tuple(
    name for name, (shape, _) in ipa_table().items() if name in POINT_NAMES or math.prod(shape) < D * D and shape[0] != D * HEADS
)


def attention_backward_body(ins, ipa, flat, outs, scratch, grads, stage, tick, head_tick, edge_ticks, grads_done):
    ipa_cot, skip_cot, frame_cot, time_ref, turn_ref, move_ref, edge_ref, edge_own = ins[:8]
    kept, wide, attend, pair_held = ins[8:12]
    node_grad, turn_grad, move_grad, edge_grad = outs
    (
        pair_c, attend_c, logit_c, time_c, query_pts_c, key_pts_c, value_pts_c, pair_sum,
        edge_held, edge_sem, head_weights, head_sem,
    ) = scratch
    slots = POINT_SLOTS
    count = time_ref.shape[0]
    held = lambda slot, width=D: kept[slot, :, 0:width]
    entries = {entry[0]: entry for entry in layout(ipa_table())}
    edge_in = pltpu.make_async_copy(edge_own, edge_held, edge_sem)
    edge_in.start()

    def weight_copies(head, slot):
        cols = pl.ds(pl.multiple_of(head * HEAD_DIM, HEAD_DIM), HEAD_DIM)
        return [
            pltpu.make_async_copy(weight.at[:, cols], head_weights.at[slot, k], head_sem.at[slot, k])
            for k, weight in enumerate((ipa.query_w, ipa.key_w, ipa.value_w))
        ]

    for copy in weight_copies(0, 0):
        copy.start()
    clear_tail(flat, ipa_table())

    def store_tiles(entry, first, value):
        _, offset, _, width, scale, _ = entry
        lines, lane = width // LANES, offset % LANES
        for place in range(value.shape[1] // LANES):
            tile = value[:, place * LANES : (place + 1) * LANES] * scale
            store_lines(flat, offset // LANES + first * lines + place, lane, lines, tile)

    def store_out(first, value):
        store_tiles(entries[OUT_NAME], first, value)

    def store_time(value):
        store_tiles(entries[TIME_NAME], 0, value)

    def store_head(place, head, value, bias):
        weight, shift = entries[HEAD_NAMES[2 * place]], entries[HEAD_NAMES[2 * place + 1]]
        for part in range(HEAD_DIM // LANES):
            cols = slice(part * LANES, (part + 1) * LANES)
            at = head * (HEAD_DIM // LANES) + part
            store_lines(flat, weight[1] // LANES + at, 0, weight[3] // LANES, value[:, cols] * weight[4])
            store_lines(flat, shift[1] // LANES + at, 0, 1, bias[:, cols] * shift[4])

    def pack_small(early=None):
        chosen = [entry for entry in entries.values() if entry[0] in SMALL_NAMES]
        last = len(chosen) - 1
        chosen = chosen[last:] if early is not None else chosen[:last]
        pack_into(flat, chosen, vars(grads), stage)

    turn, move = single_rows(rows_of(turn_ref), 3), single_rows(rows_of(move_ref), 3)
    columns = turned_over(rotation_rows(*turn) + move)
    column = [columns[:, k : k + 1] for k in range(12)]
    turn_c, move_c = column[:9], column[9:12]

    ipa_unit = held(slots.unit)
    ipa_c = affine_back(ipa.ipa_gain, grads.ipa_gain, grads.ipa_shift, ipa_unit, ipa_cot[...])
    att_c = norm_back(ipa_c, ipa_unit, kept[slots.inverse, :, 0:1])
    time_c[...] = att_c
    grads.out_b[...] = jnp.sum(att_c, 0, keepdims=True)

    point_rows = slice(SCALAR_OUT, SCALAR_OUT + POINT_ROWS)
    feats, shifted = held(slots.feats, POINT_ROWS), axis_parts(held(slots.pg, 3 * V_AXIS), V_AXIS)
    feats_c = dot_high(att_c, ipa.out_w[point_rows, :], NT)
    store_out(POINT_AT, dot_high(feats, att_c, TN))
    ratio = feats_c[:, 3 * V_AXIS :] / feats[:, 3 * V_AXIS :]
    local, local_c = axis_parts(feats, V_AXIS), axis_parts(feats_c, V_AXIS)
    local_c = [own + ratio * value for own, value in zip(local_c, local)]
    shifted_c = [
        turn_c[3 * d] * local_c[0] + turn_c[3 * d + 1] * local_c[1] + turn_c[3 * d + 2] * local_c[2]
        for d in range(3)
    ]
    over = lambda value: jnp.sum(value, -1, keepdims=True)
    turn_sums = [over(local_c[c] * shifted[d]) for d in range(3) for c in range(3)]
    move_sums = [-over(shifted_c[d]) for d in range(3)]
    points_c = jnp.concatenate(shifted_c, 1)

    def pair_back(head, _):
        rows = pl.ds(pl.multiple_of(SCALAR_OUT + POINT_ROWS + head * E, E), E)
        pair_c[head_rows(head, count), :] = dot_high(att_c, ipa.out_w[rows, :], NT)
        store_out(POINT_AT + POINT_ROWS + head * E, dot_high(pair_held[head_rows(head, count), :], att_c, TN))
        cols = pl.ds(pl.multiple_of(head * HEAD_DIM, HEAD_DIM), HEAD_DIM)
        store_out(head * HEAD_DIM, dot_high(wide[3, :, cols], att_c, TN))
        return 0

    lax.fori_loop(0, HEADS, pair_back, 0)
    pack_small(grads.out_b)
    tick(0)
    group, fold = group_mask(), group_fold(count)

    def group_rows(place):
        edges = pl.ds(pl.multiple_of(place * GROUP * 32, GROUP * 32), GROUP * 32)
        return edges, pl.ds(pl.multiple_of(place * GROUP * HEADS, GROUP * HEADS), GROUP * HEADS)

    def attend_back(place):
        edges, here = group_rows(place)
        wide_c = dot_high(pair_c[here, :], edge_ref[edges, :], NT) * group
        attend_c[here, :] = dot_marks(wide_c, fold)

    each_group(0, count // GROUP, attend_back)
    tick(1)

    node_time = held(slots.time)
    query_pts, key_pts = held(slots.gq, 3 * Q_AXIS), held(slots.gk, 3 * Q_AXIS)
    value_pts = held(slots.gv, 3 * V_AXIS)
    point_weights = softplus(ipa.head_w[...]) * POINT_SCALE
    query_pts_c[...] = jnp.zeros_like(query_pts_c)
    key_pts_c[...] = jnp.zeros_like(key_pts_c)
    value_pts_c[...] = jnp.zeros_like(value_pts_c)
    grads.pair_b[...] = jnp.zeros_like(grads.pair_b)
    grads.head_w[...] = jnp.zeros_like(grads.head_w)

    def one_head(head, _):
        cols = pl.ds(pl.multiple_of(head * HEAD_DIM, HEAD_DIM), HEAD_DIM)
        slot = head % 2

        @pl.when(head + 1 < HEADS)
        def _():
            for copy in weight_copies(head + 1, 1 - slot):
                copy.start()

        for copy in weight_copies(head, slot):
            copy.wait()
        query, key, value = (wide[k, :, cols] for k in range(3))
        weights = attend[head_rows(head, count), :]
        mixed_c = dot_high(att_c, ipa.out_w[cols, :], NT)
        value_mask = head_lanes(value_pts.shape, VPTS, head, V_AXIS)
        weights_c = dot_high(mixed_c, value, NT) + attend_c[head_rows(head, count), :]
        weights_c = weights_c + dot_high(points_c, value_pts * value_mask, NT)
        logits_c = softmax_back(weights_c, weights) * THIRD
        logit_c[head_rows(head, count), :] = logits_c
        value_c = dot_high(weights, mixed_c, TN)
        value_pts_c[...] = value_pts_c[...] + value_mask * dot_high(weights, points_c, TN)
        logits_t = logits_c.T
        query_c = dot_high(logits_c, key) * HEAD_DIM ** (-0.5)
        key_c = dot_high(logits_t, query) * HEAD_DIM ** (-0.5)

        mask = head_lanes(query_pts.shape, QPTS, head, Q_AXIS)
        point_weight = lane_pick(point_weights, head)
        row_sum, column_sum = over(logits_c), over(logits_t)
        by_key = dot_high(logits_c, key_pts) * mask
        query_own, key_own = query_pts * mask, key_pts * mask
        query_pts_c[...] = query_pts_c[...] + (2.0 * point_weight) * (by_key - row_sum * query_own)
        key_pts_c[...] = key_pts_c[...] + (2.0 * point_weight) * (
            dot_high(logits_t, query_pts) * mask - column_sum * key_own
        )
        apart = row_sum * query_own * query_own + column_sum * key_own * key_own - 2.0 * by_key * query_own
        lane = iota((1, E), 1)
        distance_sum = jnp.sum(over(apart), 0, keepdims=True)
        grads.head_w[...] = grads.head_w[...] - jnp.where(lane == head, distance_sum, 0.0)
        grads.pair_b[...] = grads.pair_b[...] + jnp.where(
            lane == head, jnp.sum(row_sum, 0, keepdims=True), 0.0
        )

        total = time_c[...]
        for place, cot in enumerate((query_c, key_c, value_c)):
            store_head(place, head, dot_high(node_time, cot, TN), jnp.sum(cot, 0, keepdims=True))
            total = total + dot_high(cot, head_weights[slot, place], NT)
        time_c[...] = total
        head_tick(head)
        return 0

    lax.fori_loop(0, HEADS, one_head, 0)
    tick(2)
    raw = ipa.head_w[...]
    grads.head_w[...] = grads.head_w[...] * (POINT_SCALE / (1.0 + jnp.exp(-raw)))

    for weight, bias, weight_g, bias_g, cot_ref, size in (
        (ipa.qpoint_w, ipa.qpoint_b, grads.qpoint_w, grads.qpoint_b, query_pts_c, Q_AXIS),
        (ipa.kpoint_w, ipa.kpoint_b, grads.kpoint_w, grads.kpoint_b, key_pts_c, Q_AXIS),
        (ipa.vpoint_w, ipa.vpoint_b, grads.vpoint_w, grads.vpoint_b, value_pts_c, V_AXIS),
    ):
        plain = dot_high(node_time, weight[:, : 3 * size]) + bias[:, : 3 * size]
        local, cot = axis_parts(plain, size), axis_parts(cot_ref[...], size)
        turn_sums = [
            turn_sums[3 * c + d] + over(cot[c] * local[d]) for c in range(3) for d in range(3)
        ]
        move_sums = [move_sums[c] + over(cot[c]) for c in range(3)]
        flat_c = [turn_c[d] * cot[0] + turn_c[3 + d] * cot[1] + turn_c[6 + d] * cot[2] for d in range(3)]
        flat_c = jnp.concatenate(flat_c, 1)
        time_c[...] = time_c[...] + linear_back(weight, weight_g, bias_g, node_time, flat_c)

    total = time_c[...]
    store_time(dot_high(time_ref[...], total, TN))
    node_grad[...] = total + skip_cot[...]

    pair_turned = ipa.pair_w[...].T[0:HEADS, :]
    pair_tiled = jnp.concatenate([pair_turned] * GROUP, 0)
    pair_sum[...] = jnp.zeros_like(pair_sum)

    def pair_weights(place):
        edges, here = group_rows(place)
        wide_l = dot_marks(logit_c[here, :], fold, NT) * group
        pair_sum[...] = pair_sum[...] + dot_high(wide_l, edge_ref[edges, :])

    each_group(0, count // GROUP, pair_weights)
    pair_total = jnp.sum(pair_sum[...].reshape(GROUP, HEADS, E), 0)
    grads.pair_w[...] = jnp.concatenate([pair_total, jnp.zeros((E - HEADS, E), jnp.float32)], 0).T
    pack_small()
    grads_done()

    def edge_back(place):
        edges, here = group_rows(place)
        wide_a = dot_marks(attend[here, :], fold, NT) * group
        wide_l = dot_marks(logit_c[here, :], fold, NT) * group
        edge_held[edges, :] = edge_held[edges, :] + (
            dot_high(wide_a, pair_c[here, :], TN) + dot_high(wide_l, pair_tiled, TN)
        )

    edge_in.wait()
    edge_ticks(lambda first, last: each_group(first, last, edge_back), count // GROUP)
    edge_done = pltpu.make_async_copy(edge_held, edge_grad, edge_sem)
    edge_done.start()

    lane = iota((count, count), 1)
    sums = sum(jnp.where(lane == k, value, 0.0) for k, value in enumerate(turn_sums + move_sums)).T
    _, turn_pull = jax.vjp(rotation_rows, *turn)
    turn_second = turn_pull(single_rows(sums, 9))
    put_rows(turn_grad, jnp.concatenate([a + b for a, b in zip(single_rows(frame_cot[...], 3), turn_second)], 0))
    put_rows(move_grad, frame_cot[3:6, :] + sums[9:12, :])
    return edge_done


def small_refs(refs):
    return SimpleNamespace(**dict(zip(SMALL_NAMES, refs)))


BODY_SCRATCH = 12


def plain_backward_kernel(*refs):
    many, few = len(IPA_ORDER), len(SMALL_NAMES)
    ins, ipa = refs[:12], named(IPA_ORDER, refs[12 : 12 + many])
    outs, flat = refs[12 + many : 16 + many], refs[16 + many]
    scratch = refs[17 + many : 17 + many + BODY_SCRATCH]
    grads, stage = small_refs(refs[17 + many + BODY_SCRATCH : -1]), refs[-1]
    nothing = lambda *_: None
    done = attention_backward_body(
        ins, ipa, flat, outs, scratch, grads, stage, nothing, nothing, lambda run, total: run(0, total), nothing
    )
    done.wait()


def scatter_backward_kernel(*refs):
    many, few = len(IPA_ORDER), len(SMALL_NAMES)
    ins, ipa, rest_flat = refs[:12], named(IPA_ORDER, refs[12 : 12 + many]), refs[12 + many]
    outs, (ipa_out, rest_out) = refs[13 + many : 17 + many], refs[17 + many : 19 + many]
    at = 19 + many
    scratch, at = refs[at : at + BODY_SCRATCH], at + BODY_SCRATCH
    grads, at = small_refs(refs[at : at + few]), at + few
    stage, flat = refs[at : at + 2]
    move = scatter_of(flat, rest_flat, refs[at + 2 :])
    move.meet()
    move.begin(0)
    move.begin(1)

    def step(place):
        for act, behind in ((move.one, 0), (move.two, 1), (move.three, 2)):
            if 0 <= place - behind < len(ROUNDS):
                act(place - behind)
        for hop in (1, 2, 3):
            if 0 <= place - 2 - hop < len(ROUNDS):
                move.line(place - 2 - hop, hop)

    def tick(place):
        if place == 2:
            move.begin(6)
            move.begin(7)
        else:
            step(place)
            move.begin(place + 2)

    def head_tick(head):
        for place, now in ((1, 2), (3, 3), (5, 4), (7, 5)):

            def act(now=now):
                step(now)
                if now < 4:
                    move.begin(now + 2)

            pl.when(head == place)(act)

    def grads_done():
        step(6)
        move.begin(8)
        move.begin(9)

    def edge_ticks(run, total):
        for place in range(7, len(ROUNDS)):
            if place < 11:
                run((place - 7) * total // 4, (place - 6) * total // 4)
            step(place)
            if place + 3 < len(ROUNDS):
                move.begin(place + 3)
        for place in range(len(ROUNDS), len(ROUNDS) + 5):
            step(place)

    done = attention_backward_body(
        ins, ipa, flat, outs, scratch, grads, stage, tick, head_tick, edge_ticks, grads_done
    )
    move.finish(ipa_out, rest_out)
    done.wait()


def in_vmem(count):
    return [pl.BlockSpec(memory_space=pltpu.VMEM)] * count


def forward_shapes(node, rotvec, trans):
    rows = node.shape[0]
    return [
        (rows, D), (rows, E), (9,) + rotvec.shape[1:], trans.shape,
        (SLOTS, rows, KEPT_WIDTH), (2 * TF_HEADS, rows, rows),
        (len(POINT_SLOTS), rows, KEPT_WIDTH), (4, rows, SCALAR_OUT), (rows * HEADS, rows), (rows * HEADS, E),
    ]


def forward_scratch(rows):
    return [
        pltpu.VMEM((rows, D), jnp.float32), pltpu.VMEM((rows, 3 * V_AXIS), jnp.float32),
        pltpu.VMEM((16, rows), jnp.float32),
    ]


def node_forward(node, times, rotvec, trans, chain, edge, mats):
    names = list(ipa_table()) + list(rest_table())[:-8]
    shapes = forward_shapes(node, rotvec, trans)
    return pl.pallas_call(
        plain_forward_kernel,
        out_shape=[jax.ShapeDtypeStruct(shape, jnp.float32) for shape in shapes],
        in_specs=in_vmem(6 + len(names)),
        out_specs=in_vmem(len(shapes)),
        scratch_shapes=forward_scratch(node.shape[0]),
        compiler_params=pltpu.CompilerParams(vmem_limit_bytes=VMEM_LIMIT),
        name="node_forward",
    )(node, times, rotvec, trans, chain, edge, *[mats[name] for name in names])


def gather_forward(ipa_params, rest_params, node, times, rotvec, trans, chain, edge):
    count = 32
    f32, dma = jnp.float32, pltpu.SemaphoreType.DMA
    ipa_rows = up_to(up_to(ipa_params.shape[0], LANES) // LANES, 8)
    rest_rows = rest_params.shape[0] // LANES
    mats = matrix_shapes(ipa_table()) + matrix_shapes(rest_table())
    shapes = forward_shapes(node, rotvec, trans)
    outs = pl.pallas_call(
        forward_kernel,
        out_shape=[jax.ShapeDtypeStruct(shape, f32) for shape in shapes + [shape for _, shape in mats]],
        in_specs=in_vmem(8),
        out_specs=in_vmem(len(shapes)) + [pl.BlockSpec(memory_space=pl.ANY)] * len(mats),
        scratch_shapes=[pltpu.VMEM(shape, f32) for _, shape in mats] + forward_scratch(node.shape[0]) + [
            pltpu.VMEM((ipa_params.shape[0] * count // LANES, LANES), f32),
            pltpu.VMEM((rest_rows * count, LANES), f32),
            pltpu.VMEM((STAGE_ROWS, LANES), f32), pltpu.VMEM((1, LANES), f32),
            dma((3, count, 4)), dma((3, count)), dma((3, count)), dma((3, count)), dma, dma, dma, dma((len(mats),)),
        ],
        compiler_params=pltpu.CompilerParams(
            collective_id=0, has_side_effects=True, vmem_limit_bytes=VMEM_LIMIT
        ),
        name="gather_forward",
    )(
        padded_rows(ipa_params, ipa_rows), rest_params.reshape(rest_rows, LANES),
        node, times, rotvec, trans, chain, edge,
    )
    return outs[: len(shapes)], dict(zip([name for name, _ in mats], outs[len(shapes) :]))


def rest_backward(cots, node, rotvec, trans, kept, probs, mats, edge_mats):
    rows = node.shape[0]
    f32 = jnp.float32
    names = list(rest_table())
    weights = [mats[name] for name in names[:-8]]
    shapes = [(rows, D), (rows, D), (8, rows), (REST_ROWS, LANES)]
    ins = [*cots, node, rotvec, trans, kept, probs, *weights, *[edge_mats[name] for name in names[-8:]]]
    return pl.pallas_call(
        rest_backward_kernel,
        out_shape=[jax.ShapeDtypeStruct(shape, f32) for shape in shapes],
        in_specs=in_vmem(len(ins)),
        out_specs=in_vmem(len(shapes)),
        scratch_shapes=[pltpu.VMEM(weight.shape, f32) for weight in weights] + [pltpu.VMEM((STAGE_ROWS, LANES), f32)],
        compiler_params=pltpu.CompilerParams(vmem_limit_bytes=VMEM_LIMIT),
        name="rest_backward",
    )(*ins)


def attention_backward(on_small, cots, times, rotvec, trans, edge, edge_own, held, mats, rest_flat):
    rows = times.shape[0]
    f32, dma = jnp.float32, pltpu.SemaphoreType.DMA
    anywhere = pl.BlockSpec(memory_space=pl.ANY)
    weights = [mats[name] for name in IPA_ORDER]
    shapes = [(rows, D), rotvec.shape, trans.shape, edge.shape]
    scratch = [
        pltpu.VMEM((rows * HEADS, E), f32), pltpu.VMEM((rows * HEADS, rows), f32),
        pltpu.VMEM((rows * HEADS, rows), f32), pltpu.VMEM((rows, D), f32),
        pltpu.VMEM((rows, 3 * Q_AXIS), f32), pltpu.VMEM((rows, 3 * Q_AXIS), f32),
        pltpu.VMEM((rows, 3 * V_AXIS), f32), pltpu.VMEM((GROUP * HEADS, E), f32),
        pltpu.VMEM(edge.shape, f32), dma,
        pltpu.VMEM((2, 3, D, HEAD_DIM), f32), dma((2, 3)),
    ]
    scratch = scratch + [pltpu.VMEM(mats[name].shape, f32) for name in SMALL_NAMES]
    scratch = scratch + [pltpu.VMEM((STAGE_ROWS, LANES), f32)]
    ins = [*cots, times, rotvec, trans, edge, edge_own, *held, *weights]
    in_specs = in_vmem(len(ins))
    for place in (7, *[len(ins) - len(weights) + IPA_ORDER.index(name) for name in HEAD_NAMES[::2]]):
        in_specs[place] = anywhere
    out_specs = in_vmem(3) + [anywhere]
    flat_shape = (IPA_ROWS, LANES)
    if on_small:
        ins, in_specs = ins + [rest_flat], in_specs + in_vmem(1)
        shapes, out_specs = shapes + [(IPA_SLOT, LANES), (467, LANES)], out_specs + in_vmem(2)
        scratch = scratch + [pltpu.VMEM(flat_shape, f32)] + scatter_scratch()
        body, params = scatter_backward_kernel, dict(collective_id=1, has_side_effects=True)
    else:
        shapes, out_specs = shapes + [flat_shape], out_specs + in_vmem(1)
        body, params = plain_backward_kernel, {}
    return pl.pallas_call(
        body,
        out_shape=[jax.ShapeDtypeStruct(shape, f32) for shape in shapes],
        in_specs=in_specs,
        out_specs=out_specs,
        scratch_shapes=scratch,
        compiler_params=pltpu.CompilerParams(vmem_limit_bytes=VMEM_LIMIT, **params),
        name="attention_backward",
    )(*ins)


def time_rows(timestep, length):
    half = D // 2
    frequency = jnp.exp(-math.log(10000.0) * jnp.arange(half, dtype=jnp.float32) / half)
    angles = timestep.astype(jnp.float32)[:, None] * frequency
    return jnp.repeat(jnp.concatenate([jnp.sin(angles), jnp.cos(angles)], -1), length, axis=0)


def on_device(
    node,
    edge,
    rotvec,
    trans,
    chain,
    timestep,
    ipa_params,
    rest_params,
    node_cot,
    edge_cot,
    rot_cot,
    trans_cot,
):
    on_small = small_slice(ipa_params, rest_params)
    crops, length = chain.shape
    rows = crops * length
    times = time_rows(timestep, length)
    nodes, edges = node.reshape(rows, D), edge.reshape(-1, E)
    turned = lambda array: jnp.transpose(array, (1, 0, 2))
    turn_in, move_in = turned(rotvec), turned(trans)
    ins = (nodes, times, turn_in, move_in, chain, edges)
    if on_small:
        outs, mats = gather_forward(ipa_params, rest_params, *ins)
    else:
        mats = unpack_all(*gather_any(ipa_params, rest_params))
        outs = node_forward(*ins, mats)
    node_out, projected, rot_out, trans_out, *held = outs
    (node_out, rot_out, trans_out, edge_out, edge_own, proj_cot), edge_mats = edge_all(
        edges, edge_cot.reshape(-1, E), projected, (node_out, rot_out, trans_out), mats
    )
    cots = (node_cot.reshape(rows, D), proj_cot, turned(rot_cot), turned(trans_cot))
    *node_cots, rest_flat = rest_backward(cots, nodes, turn_in, move_in, *held[:2], mats, edge_mats)
    node_grad, rotvec_grad, trans_grad, edge_grad, *flats = attention_backward(
        on_small, node_cots, times, turn_in, move_in, edges, edge_own, held[2:], mats, rest_flat
    )
    if on_small:
        ipa_grad, rest_grad = [flat.reshape(-1) for flat in flats]
    else:
        ipa_grad, rest_grad = scatter_any(*flats, rest_flat, ipa_params, rest_params)
    return (
        node_out.reshape(node.shape), edge_out.reshape(edge.shape), turned(rot_out), turned(trans_out),
        node_grad.reshape(node.shape), edge_grad.reshape(edge.shape), turned(rotvec_grad), turned(trans_grad),
        ipa_grad[: ipa_params.shape[0]], rest_grad,
    )


def solution(mesh):
    one, two, three, four = (P(AXES, *[None] * extra) for extra in range(4))
    return jax.shard_map(
        on_device,
        mesh=mesh,
        in_specs=(three, four, three, three, two, one, one, one, three, four, three, three),
        out_specs=(three, four, three, three, three, four, three, three, one, one),
        check_vma=False,
    )
```
